128 devices in a mesh: replica: 8 (over x, core), fsdp: 16 (over y, z).
Axes of the slice: x: 4, y: 4, z: 4, core: 2. Of those that a mesh axis runs over, the one named last changes fastest.
Arguments:
- tokens: bfloat16 [16384, 1024], P(('replica', 'fsdp')), may hold values from -6 to 6
- lengths: int32 [8, 4], P('replica'), may hold values from 1 to 2045, as said below
- cotangent: bfloat16 [16384, 1024], P(('replica', 'fsdp')), may hold values from -6 to 6
- attention_gain: bfloat16 [1024], P('fsdp'), may hold values from 0.099609375 to 1.8984375
- query_weight: bfloat16 [1024, 1024], P('fsdp'), may hold values from -0.1875 to 0.1875
- key_weight: bfloat16 [1024, 512], P('fsdp'), may hold values from -0.1875 to 0.1875
- value_weight: bfloat16 [1024, 512], P('fsdp'), may hold values from -0.1875 to 0.1875
- query_gain: bfloat16 [64], P('fsdp'), may hold values from 0.099609375 to 1.8984375
- key_gain: bfloat16 [64], P('fsdp'), may hold values from 0.099609375 to 1.8984375
- out_weight: bfloat16 [1024, 1024], P('fsdp'), may hold values from -1.5 to 1.5
- middle_gain: bfloat16 [1024], P('fsdp'), may hold values from 0.099609375 to 1.8984375
- gate_weight: bfloat16 [1024, 4608], P(None, 'fsdp'), may hold values from -0.1875 to 0.1875
- up_weight: bfloat16 [1024, 4608], P(None, 'fsdp'), may hold values from -0.1875 to 0.1875
- down_weight: bfloat16 [4608, 1024], P('fsdp'), may hold values from -0.09375 to 0.09375
Outputs:
- block_output: bfloat16 [16384, 1024], P(('replica', 'fsdp'))
- tokens_grad: float32 [16384, 1024], P(('replica', 'fsdp'))
- attention_gain_grad: float32 [1024], P('fsdp')
- query_weight_grad: float32 [1024, 1024], P('fsdp')
- key_weight_grad: float32 [1024, 512], P('fsdp')
- value_weight_grad: float32 [1024, 512], P('fsdp')
- query_gain_grad: float32 [64], P('fsdp')
- key_gain_grad: float32 [64], P('fsdp')
- out_weight_grad: float32 [1024, 1024], P('fsdp')
- middle_gain_grad: float32 [1024], P('fsdp')
- gate_weight_grad: float32 [1024, 4608], P(None, 'fsdp')
- up_weight_grad: float32 [1024, 4608], P(None, 'fsdp')
- down_weight_grad: float32 [4608, 1024], P('fsdp')
The draws below stay inside these ranges and needn't reach their ends.
Inputs may be any that keep to these rules, and one draw needn't show every extreme that they name: Each row's 4 lengths sum to 2048; all of them but one are at most 32.
All inputs are finite; a program needn't handle non-finite values.
Results may differ from the reference program's by a relative error of at most 0.025.
Values may be sent and summed in bfloat16 or wider, within the bound.
No kernel may reach another device: no remote copies, remote signals or barrier semaphores. Data moves between devices by JAX's collectives and lax.ppermute only.
A program may use at most 192 MiB of HBM per device.

```python
import math
import jax
import jax.numpy as jnp
from jax import lax

D = 1024
HEADS = 16
KV_HEADS = 8
HEAD_DIM = 64
FF = 4608
TOK_DEV = 128
SEQS = 4
GROUPS = 8
GROUP = 2048
TOKENS = 16384
HQ = 1024
HK = 512


def draw_lengths(key, part):
    key = jax.random.fold_in(key, 11)
    pick_key, short_key, group_key = jax.random.split(key, 3)
    longest = jax.random.randint(pick_key, (GROUPS, 1), 0, SEQS)
    shorts = jax.random.randint(short_key, (GROUPS, SEQS), 1, TOK_DEV // SEQS + 1)
    chosen = jax.random.randint(group_key, (), 0, GROUPS)
    rows = jnp.arange(GROUPS, dtype=jnp.int32)[:, None]
    shorts = jnp.where(rows == chosen, 1, shorts)
    slots = jnp.arange(SEQS, dtype=jnp.int32)[None, :]
    shorts = jnp.where(slots == (longest + 1) % SEQS, 1, shorts)
    shorts = jnp.where(slots == longest, 0, shorts)
    remains = GROUP - jnp.sum(shorts, axis=1, keepdims=True)
    return jnp.where(slots == longest, remains, shorts).astype(jnp.int32)


def block_levels(stream_key, extent, cuts, least, high):
    def one(dim, blocks):
        steps = jax.random.uniform(jax.random.fold_in(jax.random.fold_in(stream_key, 6), dim), (blocks,), jnp.float32, least / len(cuts), high / len(cuts))
        return jnp.repeat(jnp.exp(steps), extent[dim] // blocks).reshape((-1,) + (1,) * (len(extent) - dim - 1))

    factor_of = one(*cuts[0])
    for cut in cuts[1:]:
        factor_of = factor_of * one(*cut)
    return factor_of


def normal_values(key, shape, width, reach, cuts=(), held_as=jnp.bfloat16):
    level = block_levels(key, shape, cuts, -0.22, 0.18) if cuts else 1.0
    values = jax.random.normal(key, shape, jnp.float32) * width * level
    return jnp.minimum(jnp.maximum(values, -reach), reach).astype(held_as)


def setup_inputs(seed: int = 0) -> dict:
    splits = jax.random.split(jax.random.key(seed), 15)
    return {
        "tokens": normal_values(splits[0], (TOKENS, D), 1.0, 6.0, ((0, 128),)),
        "lengths": draw_lengths(jax.random.fold_in(splits[14], 71), 0),
        "cotangent": normal_values(splits[2], (TOKENS, D), 1.0, 6.0, ((0, 128),)),
        "attention_gain": jnp.clip(1.0 + 0.18 * jax.random.normal(splits[3], (D,), jnp.float32), 0.099609375, 1.8984375).astype(jnp.bfloat16),
        "query_weight": normal_values(splits[4], (D, HQ), D ** -0.5, 0.1875, ((0, 16),)),
        "key_weight": normal_values(splits[5], (D, HK), D ** -0.5, 0.1875, ((0, 16),)),
        "value_weight": normal_values(splits[6], (D, HK), D ** -0.5, 0.1875, ((0, 16),)),
        "query_gain": jnp.clip(1.0 + 0.18 * jax.random.normal(splits[7], (HEAD_DIM,), jnp.float32), 0.099609375, 1.8984375).astype(jnp.bfloat16),
        "key_gain": jnp.clip(1.0 + 0.18 * jax.random.normal(splits[8], (HEAD_DIM,), jnp.float32), 0.099609375, 1.8984375).astype(jnp.bfloat16),
        "out_weight": normal_values(splits[9], (HQ, D), (max(HQ // 64, 1)) ** -0.5, 1.5, ((0, 16),)),
        "middle_gain": jnp.clip(1.0 + 0.18 * jax.random.normal(splits[10], (D,), jnp.float32), 0.099609375, 1.8984375).astype(jnp.bfloat16),
        "gate_weight": normal_values(splits[11], (D, FF), D ** -0.5, 0.1875, ((1, 16),)),
        "up_weight": normal_values(splits[12], (D, FF), D ** -0.5, 0.1875, ((1, 16),)),
        "down_weight": normal_values(splits[13], (FF, D), FF ** -0.5, 0.09375, ((0, 16),)),
    }


epsilon = 1e-05
rope_base = 1000000.0
masked_score = -1e+30

@jax.custom_vjp
def low(v):
    return lax.optimization_barrier(v.astype(jnp.bfloat16)).astype(jnp.float32)

@jax.custom_vjp
def low_back(v):
    return v

def low_keep(v):
    return (low(v), None)

def low_pass(kept, grad):
    return (grad,)

def back_keep(v):
    return (v, None)

def back_low(kept, grad):
    return (low(grad),)
low.defvjp(low_keep, low_pass)
low_back.defvjp(back_keep, back_low)

def rms_scale(source, gain):
    return source * lax.rsqrt(lax.optimization_barrier(jnp.mean(source * source, axis=-1, keepdims=True)) + epsilon) * gain

def rotate(source, cosine, sine):
    middle_at = source.shape[-1] // 2
    first_half = source[..., :middle_at]
    second_half = source[..., middle_at:]
    return jnp.concatenate([first_half * cosine - second_half * sine, second_half * cosine + first_half * sine], axis=-1)

def tables(position):
    steps_half = jnp.arange(HEAD_DIM // 2, dtype=jnp.float32)
    inverse = rope_base ** (-2.0 * steps_half / HEAD_DIM)
    angles = position.astype(jnp.float32)[:, None] * inverse[None, :]
    return (jnp.cos(angles)[:, None, :], jnp.sin(angles)[:, None, :])

def layout(seq_lengths):
    ends = jnp.cumsum(seq_lengths).astype(jnp.int32)
    places = jnp.arange(GROUP, dtype=jnp.int32)
    passed = (places[:, None] >= ends[None, :]).astype(jnp.int32)
    document = lax.optimization_barrier(jnp.sum(passed, axis=1)).astype(jnp.int32)
    position = (places - lax.optimization_barrier(jnp.sum(passed * seq_lengths[None, :], axis=1))).astype(jnp.int32)
    return (document, position)

def attend(queries, keys, values, document):
    block_rows = math.gcd(512, GROUP)
    repeat = HEADS // KV_HEADS
    places = jnp.arange(GROUP, dtype=jnp.int32)

    def one_block(block_start):
        query_block = lax.dynamic_slice_in_dim(queries, block_start, block_rows, 0).reshape(block_rows, KV_HEADS, repeat, HEAD_DIM)
        query_doc = lax.dynamic_slice_in_dim(document, block_start, block_rows, 0)
        query_place = block_start + jnp.arange(block_rows, dtype=jnp.int32)
        visible = (query_doc[:, None] == document[None, :]) & (places[None, :] <= query_place[:, None])
        scores = low_back(jnp.einsum('tgrd,jgd->tgrj', query_block, keys, precision=lax.Precision.HIGHEST) * HEAD_DIM ** (-0.5))
        masked = jnp.where(visible[:, None, None, :], scores, masked_score)
        largest = lax.optimization_barrier(jnp.max(masked, axis=-1, keepdims=True))
        weights = jnp.exp(masked - largest)
        probs = weights / lax.optimization_barrier(jnp.sum(weights, axis=-1, keepdims=True))
        mixed_rows = jnp.einsum('tgrj,jgd->tgrd', low(probs), values, precision=lax.Precision.HIGHEST)
        return mixed_rows.reshape(block_rows, HEADS * HEAD_DIM)
    block_starts = jnp.arange(GROUP // block_rows, dtype=jnp.int32) * block_rows
    return lax.map(jax.checkpoint(one_block), block_starts).reshape(GROUP, HEADS * HEAD_DIM)

def forward(inputs, attention_gain, query_weight, key_weight, value_weight, query_gain, key_gain, out_weight, middle_gain, gate_weight, up_weight, down_weight, document, cosine, sine):
    highest = lax.Precision.HIGHEST
    normed_in = low(rms_scale(inputs, attention_gain))
    query_raw = low_back(jnp.dot(normed_in, query_weight, precision=highest))
    key_raw = low_back(jnp.dot(normed_in, key_weight, precision=highest))
    values = low(low_back(jnp.dot(normed_in, value_weight, precision=highest))).reshape(TOKENS, KV_HEADS, HEAD_DIM)
    queries = low(rotate(rms_scale(query_raw.reshape(TOKENS, HEADS, HEAD_DIM), query_gain), cosine, sine))
    keys = low(rotate(rms_scale(key_raw.reshape(TOKENS, KV_HEADS, HEAD_DIM), key_gain), cosine, sine))
    grouped = (queries.reshape(GROUPS, GROUP, HEADS, HEAD_DIM), keys.reshape(GROUPS, GROUP, KV_HEADS, HEAD_DIM), values.reshape(GROUPS, GROUP, KV_HEADS, HEAD_DIM), document)
    attended = lax.map(lambda pieces: attend(pieces[0], pieces[1], pieces[2], pieces[3]), grouped)
    attended = low(low_back(attended.reshape(TOKENS, HEADS * HEAD_DIM)))
    middle = inputs + low_back(jnp.dot(attended, out_weight, precision=highest))
    normed_mid = low(rms_scale(middle, middle_gain))
    gate_rows = low_back(jnp.dot(normed_mid, gate_weight, precision=highest))
    up_rows = low_back(jnp.dot(normed_mid, up_weight, precision=highest))
    hidden = low(jax.nn.silu(gate_rows) * up_rows)
    return middle + low_back(jnp.dot(hidden, down_weight, precision=highest))

def reference(tokens, lengths, cotangent, attention_gain, query_weight, key_weight, value_weight, query_gain, key_gain, out_weight, middle_gain, gate_weight, up_weight, down_weight):
    document, position = jax.vmap(layout)(lengths)
    cosine, sine = tables(position.reshape(TOKENS))
    params = (attention_gain, query_weight, key_weight, value_weight, query_gain, key_gain, out_weight, middle_gain, gate_weight, up_weight, down_weight)
    params = tuple((item.astype(jnp.float32) for item in params))

    def run(inputs, *weights):
        return forward(inputs, *weights, document, cosine, sine)
    output, pullback = jax.vjp(run, tokens.astype(jnp.float32), *params)
    grads = pullback(cotangent.astype(jnp.float32))
    return (output.astype(jnp.bfloat16), grads[0], grads[1], grads[2], grads[3], grads[4], grads[5], grads[6], grads[7], grads[8], grads[9], grads[10], grads[11])
```

```python
import functools

import jax
import jax.numpy as jnp
import numpy as np
from jax import lax
from jax.experimental import pallas as pl
from jax.experimental.pallas import tpu as pltpu
from jax.sharding import PartitionSpec as P

F32 = jnp.float32
BF16 = jnp.bfloat16
EPS = 1e-05
ROPE_BASE = 1000000.0
HEAD_DIM = 64


def shape(dims, dtype):
    return jax.ShapeDtypeStruct(dims, dtype)


def run(kernel, outs, args, scratch=()):
    at, rest = args[0], args[1:]
    return pl.pallas_call(
        kernel,
        out_shape=[shape(dims, dtype) for dims, dtype in outs],
        in_specs=[pl.BlockSpec(memory_space=pltpu.SMEM)]
        + [pl.BlockSpec(memory_space=pltpu.VMEM)] * len(rest),
        out_specs=[pl.BlockSpec(memory_space=pltpu.VMEM)] * len(outs),
        scratch_shapes=list(scratch),
        compiler_params=pltpu.CompilerParams(vmem_limit_bytes=50 * 1024 * 1024),
    )(at, *rest)


def yz_perm(dy, dz):
    return [
        (y * 4 + z, ((y + dy) % 4) * 4 + (z + dz) % 4) for y in range(4) for z in range(4)
    ]


def to_y(value, step):
    return lax.ppermute(value, "fsdp", yz_perm(step, 0))


def to_z(value, step):
    return lax.ppermute(value, "fsdp", yz_perm(0, step))


def to_x(value, step):
    pairs = [(x * 2 + c, ((x + step) % 4) * 2 + c) for x in range(4) for c in range(2)]
    return lax.ppermute(value, "replica", pairs)


def to_core(value):
    return lax.ppermute(value, "replica", [(i, i ^ 1) for i in range(8)])


def gather(move, own):
    return [own] + [move(own, step) for step in (1, 2, 3)]


def scatter(move, blocks):
    return [blocks[0]] + [move(blocks[step], -step) for step in (1, 2, 3)]


def back(place, step):
    return lax.rem(place - step + 4, 4)


def ahead(place, step):
    return lax.rem(place + step, 4)


def rows_at(start, count):
    return pl.ds(pl.multiple_of(start, count), count)


def nt(left, right):
    return lax.dot_general(left, right, (((1,), (1,)), ((), ())), preferred_element_type=F32)


def nn(left, right):
    return jnp.dot(left, right, preferred_element_type=F32)


def lane_of(value):
    return lax.broadcasted_iota(jnp.int32, value.shape, value.ndim - 1)


def low_lanes(value):
    return lane_of(value) < HEAD_DIM


def swap_halves(value):
    first = lax.rem(lane_of(value), HEAD_DIM) < HEAD_DIM // 2
    return jnp.where(first, pltpu.roll(value, 96, 1), pltpu.roll(value, 32, 1))


def head_mean(value):
    low = low_lanes(value)
    left = jnp.sum(jnp.where(low, value, 0.0), axis=1, keepdims=True)
    right = jnp.sum(jnp.where(low, 0.0, value), axis=1, keepdims=True)
    return jnp.where(low, left, right) * (1.0 / HEAD_DIM)


def head_forward(raw, gain, cosine, sine):
    normed = raw * lax.rsqrt(head_mean(raw * raw) + EPS) * gain
    return normed * cosine + swap_halves(normed) * sine


def head_backward(grad, raw, gain, cosine, sine):
    turned = grad * cosine - swap_halves(grad) * sine
    scale = lax.rsqrt(head_mean(raw * raw) + EPS)
    scaled = turned * gain
    d_raw = scale * scaled - raw * (scale * scale * scale) * head_mean(scaled * raw)
    return d_raw, jnp.sum(turned * raw * scale, axis=0, keepdims=True)


def gain_rows(tile):
    row = tile[0:8, :]
    turned = pltpu.roll(row, 64, 1)
    low = low_lanes(row)
    return jnp.where(low, row, turned)[0:1], jnp.where(low, turned, row)[0:1]


def middle_gain_row(tile):
    return jnp.concatenate([tile[8 + i : 9 + i, :] for i in range(8)], axis=1)


def stack_heads(tile, group):
    low = low_lanes(tile)
    turned = pltpu.roll(tile, 64, 1)
    if group == 0:
        pair = [jnp.where(low, tile, 0.0), jnp.where(low, turned, 0.0)]
    else:
        pair = [jnp.where(low, 0.0, turned), jnp.where(low, 0.0, tile)]
    return jnp.concatenate(pair, axis=0).astype(BF16)


def unstack_heads(stacked, group):
    top, bottom = stacked[0:128], stacked[128:256]
    low = low_lanes(top)
    if group == 0:
        return jnp.where(low, top, pltpu.roll(bottom, 64, 1))
    return jnp.where(low, pltpu.roll(top, 64, 1), bottom)


def visible_part(part, starts, place, last):
    key_place = lax.broadcasted_iota(jnp.int32, (512, 256), 0) + part * 512
    seen = key_place >= starts
    return seen & (key_place <= place) if last else seen


def row_places(block, z, starts_ref):
    place = (4 * block + z) * 128 + lax.broadcasted_iota(jnp.int32, (1, 128), 1)
    start = starts_ref[block : block + 1, :]
    return jnp.concatenate([place, place], axis=1), jnp.concatenate([start, start], axis=1)


def prepare(at, gains, rows, w_q, w_k, w_v, normed, *sends):
    y, z = at[0], at[1]
    place = 4 * y + z
    source = rows[...].astype(F32)
    scale = lax.rsqrt(jnp.mean(source * source, axis=1, keepdims=True) + EPS)
    normed[...] = (source * scale).astype(BF16)
    held = gains[...]
    lane = lax.broadcasted_iota(jnp.int32, (64, 128), 1)
    line = lax.broadcasted_iota(jnp.int32, (64, 128), 0)
    column = jnp.sum(jnp.where(lane == line, held[0:1, :], 0.0), axis=1, keepdims=True)
    heads = pltpu.roll(held, 4 * place, 1)[2:3] + pltpu.roll(held, 64 + 4 * place, 1)[3:4]
    middle = pltpu.roll(held, 64 * lax.rem(place, 2), 1)[1:2]
    line = lax.broadcasted_iota(jnp.int32, (16, 128), 0)
    tile = jnp.where(line == 0, heads, 0.0) + jnp.where(line == 8 + place // 2, middle, 0.0)
    for step in range(4):
        other = ahead(y, step)
        send = sends[step]
        for source_ref, width, first in ((w_q, 256, 0), (w_k, 128, 256), (w_v, 128, 384)):
            block = source_ref[:, rows_at(other * width, width)].astype(F32) * column
            send[0:64, first : first + width] = block.astype(BF16)
        send[64:80, 0:128] = tile.astype(BF16)
        send[64:80, 128:512] = jnp.zeros((16, 384), BF16)


def project(at, *refs):
    x_parts, w_parts = refs[0:4], refs[4:8]
    cosine_ref, sine_ref = refs[8:10]
    query, key_value, raw, x_full, w_full, gain_tile = refs[10:]
    y, z = at[0], at[1]
    total = jnp.zeros((16, 128), F32)
    for step in range(4):
        x_full[rows_at(back(y, step) * 128, 128), :] = x_parts[step][...]
        for inner in range(4):
            place = back(y, inner) * 4 + back(z, step)
            first = inner * 80
            w_full[rows_at(place * 64, 64), :] = w_parts[step][first : first + 64, :]
            total = total + w_parts[step][first + 64 : first + 80, 0:128].astype(F32)
    gain_tile[...] = total
    gain_q, gain_k = gain_rows(total)
    cosine, sine = cosine_ref[...], sine_ref[...]
    product = nn(x_full[...], w_full[...])
    raw[...] = product[:, 0:384]
    for tile in range(2):
        part = product[:, tile * 128 : tile * 128 + 128]
        turned = head_forward(part, gain_q, cosine, sine) * (HEAD_DIM**-0.5)
        query[:, tile * 128 : tile * 128 + 128] = turned.astype(BF16)
    key_value[:, 0:128] = head_forward(product[:, 256:384], gain_k, cosine, sine).astype(BF16)
    key_value[:, 128:256] = product[:, 384:512].astype(BF16)


def attend(at, query, *refs):
    kv_parts, out_parts, starts = refs[0:4], refs[4:8], refs[8]
    keys, values, attended, inverse, w_out = refs[9:14]
    partials, (values_t, mixed) = refs[14:18], refs[18:]
    y, z = at[0], at[1]
    for step in range(4):
        other = back(z, step)
        for block in range(4):
            rows = kv_parts[step][block * 128 : block * 128 + 128, :]
            target = rows_at((4 * block + other) * 128, 128)
            keys[target, :] = rows[:, 0:128]
            values[target, :] = rows[:, 128:256]
        w_out[rows_at(other * 64, 64), :] = out_parts[step][...]
    for part in range(4):
        chunk = values[part * 512 : part * 512 + 512, :].astype(F32)
        values_t[:, part * 512 : part * 512 + 512] = chunk.T.astype(BF16)
    for block in range(4):
        place, start = row_places(block, z, starts)
        rows = slice(block * 128, block * 128 + 128)
        for group in range(2):
            lanes = slice(group * 128, group * 128 + 128)
            stacked = stack_heads(query[rows, lanes].astype(F32), group)
            total = jnp.zeros((1, 256), F32)
            mix = jnp.zeros((128, 256), F32)
            for part in range(block + 1):
                span = slice(part * 512, part * 512 + 512)
                scores = nt(keys[span, :], stacked)
                seen = visible_part(part, start, place, part == block)
                weights = jnp.where(seen, jnp.exp(scores), 0.0)
                total = total + jnp.sum(weights, axis=0, keepdims=True)
                mix = mix + nn(values_t[:, span], weights.astype(BF16))
            share = 1.0 / total
            inverse[block * 2 + group : block * 2 + group + 1, :] = share
            attended[rows, lanes] = unstack_heads((mix * share).T, group).astype(BF16)
    mixed[...] = nn(attended[...], w_out[...])
    for step in range(4):
        partials[step][...] = mixed[rows_at(back(y, step) * 128, 128), :].astype(BF16)


def sum_parts(parts):
    total = parts[0][...].astype(F32)
    for part in parts[1:]:
        total = total + part[...].astype(F32)
    return total


def join_middle(at, rows, gain_tile, *refs):
    parts, (middle, normed) = refs[0:4], refs[4:]
    total = rows[...].astype(F32) + sum_parts(parts)
    middle[...] = total
    scale = lax.rsqrt(jnp.mean(total * total, axis=1, keepdims=True) + EPS)
    normed[...] = (total * scale * middle_gain_row(gain_tile[...])).astype(BF16)


def back_middle(at, middle, cotangent, gain_tile, *refs):
    parts, (d_middle, d_low, gain_grad) = refs[0:4], refs[4:]
    grad = sum_parts(parts)
    source = middle[...]
    scale = lax.rsqrt(jnp.mean(source * source, axis=1, keepdims=True) + EPS)
    scaled = grad * middle_gain_row(gain_tile[...])
    share = jnp.mean(scaled * source, axis=1, keepdims=True)
    total = cotangent[...].astype(F32) + scale * scaled - source * (scale**3 * share)
    d_middle[...] = total
    d_low[...] = total.astype(BF16)
    line = jnp.sum(grad * source * scale, axis=0, keepdims=True)
    gain_grad[...] = jnp.broadcast_to(line, (8, 1024))


def attend_back(at, query, keys, values, attended, inverse, w_out, starts, *refs):
    d_parts, (raw, cosine_ref, sine_ref, gain_tile) = refs[0:4], refs[4:8]
    d_kv, (d_query, gain_grad, out_grad) = refs[8:12], refs[12:15]
    d_rows, d_keys, d_values, keys_t, d_mixed = refs[15:]
    y, z = at[0], at[1]
    for step in range(4):
        d_rows[rows_at(back(y, step) * 128, 128), :] = d_parts[step][...]
    d_mixed[...] = nt(d_rows[...], w_out[...]).astype(BF16).astype(F32)
    for part in range(4):
        span = slice(part * 512, part * 512 + 512)
        keys_t[:, span] = keys[span, :].astype(F32).T.astype(BF16)
    d_keys[...] = jnp.zeros((2048, 128), F32)
    d_values[...] = jnp.zeros((2048, 128), F32)
    gain_q, _ = gain_rows(gain_tile[...])
    line = jnp.zeros((1, 128), F32)
    for block in range(4):
        place, start = row_places(block, z, starts)
        rows = slice(block * 128, block * 128 + 128)
        for group in range(2):
            lanes = slice(group * 128, group * 128 + 128)
            stacked = stack_heads(query[rows, lanes].astype(F32), group)
            d_tile = d_mixed[rows, lanes]
            d_stacked = stack_heads(d_tile, group)
            product = (d_tile * attended[rows, lanes].astype(F32)).T
            delta = jnp.concatenate(
                [
                    jnp.sum(product[0:64], axis=0, keepdims=True),
                    jnp.sum(product[64:128], axis=0, keepdims=True),
                ],
                axis=1,
            )
            share = inverse[block * 2 + group : block * 2 + group + 1, :]
            d_turned = jnp.zeros((128, 256), F32)
            for part in range(block + 1):
                span = slice(part * 512, part * 512 + 512)
                scores = nt(keys[span, :], stacked)
                seen = visible_part(part, start, place, part == block)
                probs = jnp.where(seen, jnp.exp(scores) * share, 0.0)
                d_probs = nt(values[span, :], d_stacked)
                d_scores = (probs * (d_probs - delta)).astype(BF16)
                d_values[span, :] += nn(probs.astype(BF16), d_stacked)
                d_keys[span, :] += nn(d_scores, stacked)
                d_turned = d_turned + nn(keys_t[:, span], d_scores)
            d_head = unstack_heads(d_turned.T, group) * (HEAD_DIM**-0.5)
            d_raw, gain_part = head_backward(
                d_head, raw[rows, lanes], gain_q, cosine_ref[rows, :], sine_ref[rows, :]
            )
            d_query[rows, lanes] = d_raw.astype(BF16)
            line = line + gain_part
    for step in range(4):
        other = back(z, step)
        for block in range(4):
            source = rows_at((4 * block + other) * 128, 128)
            rows = slice(block * 128, block * 128 + 128)
            d_kv[step][rows, 0:128] = d_keys[source, :].astype(BF16)
            d_kv[step][rows, 128:256] = d_values[source, :].astype(BF16)
    wide = jnp.broadcast_to(line, (8, 128))
    gain_grad[...] = wide + pltpu.roll(wide, 64, 1)
    out_grad[...] = nn(attended[...].astype(F32).T.astype(BF16), d_rows[...])


def weight_back(at, raw, cosine, sine, gain_tile, d_query, query_gain, middle_gain, *refs):
    parts, (x_full, out_grad) = refs[0:4], refs[4:6]
    d_joint, keep, send = refs[6:9]
    grads, extras = refs[9:]
    z, core = at[1], at[3]
    total = sum_parts(parts)
    _, gain_k = gain_rows(gain_tile[...])
    d_key, key_line = head_backward(
        total[:, 0:128], raw[:, 256:384], gain_k, cosine[...], sine[...]
    )
    d_joint[:, 0:256] = d_query[...]
    d_joint[:, 256:384] = d_key.astype(BF16)
    d_joint[:, 384:512] = total[:, 128:256].astype(BF16)
    wide = jnp.broadcast_to(key_line, (8, 128))
    wide = wide + pltpu.roll(wide, 64, 1)
    line = lax.broadcasted_iota(jnp.int32, (16, 128), 0)
    heads_q = jnp.concatenate([query_gain[...], query_gain[...]], axis=0)
    heads_k = jnp.concatenate([wide, wide], axis=0)
    for place in range(16):
        half = middle_gain[0:8, (place // 2) * 128 : (place // 2) * 128 + 128]
        half = jnp.concatenate([half, half], axis=0)
        if place % 2:
            half = pltpu.roll(half, 64, 1)
        turn = (128 - 4 * place) % 128
        tile = jnp.where(line == 0, half, 0.0)
        tile = tile + jnp.where(line == 1, pltpu.roll(heads_q, turn, 1) if turn else heads_q, 0.0)
        tile = tile + jnp.where(line == 2, pltpu.roll(heads_k, turn, 1) if turn else heads_k, 0.0)
        extras[place * 16 : place * 16 + 16, :] = tile
    grads[...] = lax.dot_general(
        x_full[...], d_joint[...], (((0,), (0,)), ((), ())), preferred_element_type=F32
    )
    for target, which in ((send, 1 - core), (keep, core)):
        for step in range(4):
            other = back(z, step)
            for block in range(4):
                place = block * 4 + other
                first = block * 80
                target[step, first : first + 64, :] = grads[
                    rows_at(place * 64, 64), rows_at(which * 256, 256)
                ].astype(BF16)
                target[step, first + 64 : first + 80, 0:128] = extras[
                    rows_at(place * 16, 16), :
                ].astype(BF16)
                target[step, first + 64 : first + 80, 128:256] = jnp.zeros((16, 128), BF16)
            for column in range(2):
                first = 320 + 64 * column
                target[step, first : first + 64, :] = out_grad[
                    rows_at(other * 64, 64), rows_at(which * 512 + column * 256, 256)
                ].astype(BF16)


def input_back(at, d_joint, w_full, *refs):
    blocks, (total,) = refs[0:4], refs[4:]
    y = at[0]
    total[...] = nt(d_joint[...], w_full[...])
    for step in range(4):
        blocks[step][...] = total[rows_at(back(y, step) * 128, 128), :].astype(BF16)


def join_tokens(at, rows, d_middle, *refs):
    parts, (out,) = refs[0:4], refs[4:]
    grad = sum_parts(parts)
    source = rows[...].astype(F32)
    scale = lax.rsqrt(jnp.mean(source * source, axis=1, keepdims=True) + EPS)
    share = jnp.mean(grad * source, axis=1, keepdims=True)
    out[...] = d_middle[...] + scale * grad - source * (scale**3 * share)


def tail_core(at, keep, received, *outs):
    for step in range(4):
        outs[step][...] = (keep[step].astype(F32) + received[step].astype(F32)).astype(BF16)


def tail_z(at, *refs):
    parts, blocks, out_rows, total = refs[0:4], refs[4:8], refs[8], refs[9]
    y = at[0]
    total[...] = sum_parts(parts)
    for step in range(4):
        blocks[step][...] = total[rows_at(back(y, step) * 80, 80), :].astype(BF16)
    out_rows[...] = total[320:448, :].astype(BF16)


def tail_x(at, own, one, two, three, out):
    even = own[...].astype(F32) + two[...].astype(F32)
    odd = one[...].astype(F32) + three[...].astype(F32)
    out[...] = (even + odd).astype(BF16)


def tail_out(at, own, other, gains, w_q, w_k, w_v, g_q, g_k, g_v, g_out, g_gain):
    y, core = at[0], at[3]
    own_low = core == 0
    first = jnp.where(own_low, own[...].astype(F32), other[...].astype(F32))
    second = jnp.where(own_low, other[...].astype(F32), own[...].astype(F32))
    lane = lax.broadcasted_iota(jnp.int32, (64, 128), 1)
    line = lax.broadcasted_iota(jnp.int32, (64, 128), 0)
    column = jnp.sum(jnp.where(lane == line, gains[0:1, :], 0.0), axis=1, keepdims=True)
    products = jnp.zeros((64, 128), F32)
    extra = jnp.zeros((16, 128), F32)
    for step in range(4):
        group = ahead(y, step)
        top = step * 80
        extra = extra + first[top + 64 : top + 80, 0:128]
        for source, left, width, weight, grad in (
            (first, 0, 256, w_q, g_q),
            (second, 0, 128, w_k, g_k),
            (second, 128, 128, w_v, g_v),
        ):
            block = source[top : top + 64, left : left + width]
            where = rows_at(group * width, width)
            grad[:, where] = block * column
            product = block * weight[:, where].astype(F32)
            for tile in range(width // 128):
                products = products + product[:, tile * 128 : tile * 128 + 128]
    g_out[:, 0:256] = first[320:384]
    g_out[:, 256:512] = first[384:448]
    g_out[:, 512:768] = second[320:384]
    g_out[:, 768:1024] = second[384:448]
    sums = jnp.sum(products, axis=1, keepdims=True)
    row = jnp.sum(jnp.where(lane == line, sums, 0.0), axis=0, keepdims=True)
    g_gain[0:8, :] = jnp.broadcast_to(row, (8, 128))
    g_gain[8:24, :] = extra


def ffn_core(at, keep_a, got_a, keep_b, got_b, *outs):
    x = at[2]
    step_now = pl.program_id(0)

    def write(keep, got):
        for step in range(4):
            where = rows_at(back(x, step) * 128, 128)
            outs[step][...] = (
                keep[:, where].astype(F32) + got[:, where].astype(F32)
            ).astype(BF16)

    @pl.when(step_now < 8)
    def _():
        write(keep_a, got_a)

    @pl.when(step_now >= 8)
    def _():
        write(keep_b, got_b)


def ffn_core_call(at, keep_a, got_a, keep_b, got_b):
    spec_a = pl.BlockSpec((288, 512), lambda i: (jnp.minimum(i, 7), 0))
    spec_b = pl.BlockSpec((288, 512), lambda i: (jnp.maximum(i - 8, 0), 0))
    return pl.pallas_call(
        ffn_core,
        out_shape=[shape((3456, 128), BF16)] * 4,
        grid=(12,),
        in_specs=[pl.BlockSpec(memory_space=pltpu.SMEM), spec_a, spec_a, spec_b, spec_b],
        out_specs=[pl.BlockSpec((288, 128), lambda i: (i, 0))] * 4,
        compiler_params=pltpu.CompilerParams(vmem_limit_bytes=50 * 1024 * 1024),
    )(at, keep_a, got_a, keep_b, got_b)


def ffn_x(at, *refs):
    parts, outs = refs[0:4], refs[4:8]
    for section in range(3):
        for piece in range(4):
            first = section * 1152 + piece * 288
            total = parts[0][first : first + 288, :].astype(F32)
            for part in parts[1:]:
                total = total + part[first : first + 288, :].astype(F32)
            outs[piece][section * 288 : section * 288 + 288, :] = total.astype(BF16)


def ffn_z(at, *refs):
    refs[4][...] = sum_parts(refs[0:4]).astype(BF16)


def ffn_join(at, *refs):
    parts, out = refs[0:4], refs[4]
    x = at[2]
    for step in range(4):
        out[:, rows_at(back(x, step) * 128, 128)] = parts[step][...]


def ffn_out(at, own, other, *outs):
    core = at[3]
    for section in range(3):
        rows = slice(section * 288, section * 288 + 288)
        outs[section][:, rows_at(core * 512, 512)] = own[rows, :].astype(F32)
        outs[section][:, rows_at((1 - core) * 512, 512)] = other[rows, :].astype(F32)


def on_device(
    tokens,
    lengths,
    cotangent,
    attention_gain,
    query_weight,
    key_weight,
    value_weight,
    query_gain,
    key_gain,
    out_weight,
    middle_gain,
    gate_weight,
    up_weight,
    down_weight,
):
    place = lax.axis_index("fsdp")
    copy = lax.axis_index("replica")
    y, z, x, core = place // 4, place % 4, copy // 2, copy % 2
    at = jnp.stack([y, z, x, core]).astype(jnp.int32)

    def line_of(gain):
        return jnp.pad(gain.astype(F32), (0, 128 - gain.shape[0]))[None, :]

    gains = jnp.concatenate(
        [line_of(attention_gain), line_of(middle_gain), line_of(query_gain), line_of(key_gain)]
        + [jnp.zeros((4, 128), F32)],
        axis=0,
    )

    normed, *sends = run(
        prepare,
        [((128, 1024), BF16)] + [((80, 512), BF16)] * 4,
        (at, gains, tokens, query_weight, key_weight, value_weight),
    )
    w_rows = jnp.concatenate(
        [sends[0]] + [to_y(sends[step], step) for step in (1, 2, 3)], axis=0
    )
    x_parts = gather(to_y, normed)
    w_parts = gather(to_z, w_rows)
    out_parts = gather(to_z, out_weight)
    ct_parts = gather(to_y, cotangent)

    ffn_own = jnp.concatenate([gate_weight.T, up_weight.T, down_weight], axis=0)
    ffn_parts = gather(to_z, ffn_own)
    w_gate, w_up, w_down = (
        jnp.concatenate([part[i * 288 : i * 288 + 288] for part in ffn_parts], axis=0)
        for i in range(3)
    )

    lane = np.arange(128)
    inverse_period = ROPE_BASE ** (-2.0 * (lane % 32) / HEAD_DIM)
    sign = np.where(lane % 64 < 32, -1.0, 1.0)
    blocks = jnp.arange(512, dtype=jnp.int32)
    places = (blocks // 128 * 4 + z) * 128 + blocks % 128
    passed_rows = jnp.zeros_like(places)
    end = jnp.zeros((), jnp.int32)
    for i in range(4):
        end = end + lengths[0, i]
        passed_rows = passed_rows + jnp.where(places >= end, lengths[0, i], 0)
    starts = jnp.pad(passed_rows.reshape(4, 128), ((0, 4), (0, 0)))
    angles = (places - passed_rows).astype(F32)[:, None] * jnp.asarray(inverse_period, F32)
    cosine = jnp.cos(angles)
    sine = jnp.sin(angles) * jnp.asarray(sign, F32)

    query, key_value, raw, x_full, w_full, gain_tile = run(
        project,
        [
            ((512, 256), BF16),
            ((512, 256), BF16),
            ((512, 384), F32),
            ((512, 1024), BF16),
            ((1024, 512), BF16),
            ((16, 128), F32),
        ],
        (at, *x_parts, *w_parts, cosine, sine),
    )
    kv_parts = gather(to_z, key_value)
    keys, values, attended, inverse, w_out, *mixed = run(
        attend,
        [
            ((2048, 128), BF16),
            ((2048, 128), BF16),
            ((512, 256), BF16),
            ((8, 256), F32),
            ((256, 1024), BF16),
        ]
        + [((128, 1024), BF16)] * 4,
        (at, query, *kv_parts, *out_parts, starts),
        [pltpu.VMEM((128, 2048), BF16), pltpu.VMEM((512, 1024), F32)],
    )
    middle, normed_mid = run(
        join_middle,
        [((128, 1024), F32), ((128, 1024), BF16)],
        (at, tokens, gain_tile, *scatter(to_y, mixed)),
    )

    mid_full = jnp.concatenate(gather(to_y, normed_mid), axis=0)
    ct_full = jnp.concatenate(ct_parts, axis=0)
    gate = nt(mid_full, w_gate)
    up = nt(mid_full, w_up)
    d_hidden = nt(ct_full, w_down)
    sigmoid = 1.0 / (1.0 + jnp.exp(-gate))
    silu = gate * sigmoid
    hidden = (silu * up).astype(BF16)
    d_gate = (d_hidden * up * sigmoid * (1.0 + gate * (1.0 - sigmoid))).astype(BF16)
    d_up = (d_hidden * silu).astype(BF16)
    d_normed = (nn(d_gate, w_gate) + nn(d_up, w_up)).astype(BF16)
    d_normed_parts = scatter(to_y, [d_normed[i * 128 : i * 128 + 128] for i in range(4)])
    d_middle, d_low, middle_line = run(
        back_middle,
        [((128, 1024), F32), ((128, 1024), BF16), ((8, 1024), F32)],
        (at, middle, cotangent, gain_tile, *d_normed_parts),
    )
    d_low_parts = gather(to_y, d_low)

    result = nn(hidden, w_down).astype(BF16)
    result_parts = scatter(to_y, [result[i * 128 : i * 128 + 128] for i in range(4)])
    block_output = (middle + sum_parts(result_parts)).astype(BF16)

    def halves(value):
        return [
            lax.dynamic_slice_in_dim(value, which * 512, 512, 1) for which in (1 - core, core)
        ]

    def tn(left, right):
        product = lax.dot_general(
            left, right, (((0,), (0,)), ((), ())), preferred_element_type=F32
        )
        return product.astype(BF16)

    d_both = jnp.concatenate([d_gate, d_up], axis=1)
    mid_send, mid_keep = halves(mid_full)
    ct_send, ct_keep = halves(ct_full)
    got_a = to_core(tn(d_both, mid_send))
    got_b = to_core(tn(hidden, ct_send))
    ffn_split = ffn_core_call(at, tn(d_both, mid_keep), got_a, tn(hidden, ct_keep), got_b)
    ffn_rows = run(ffn_x, [((864, 128), BF16)] * 4, (at, *scatter(to_x, ffn_split)))
    (ffn_sum,) = run(ffn_z, [((864, 128), BF16)], (at, *scatter(to_z, ffn_rows)))
    (ffn_half,) = run(ffn_join, [((864, 512), BF16)], (at, *gather(to_x, ffn_sum)))
    g_gate, g_up, g_down = run(
        ffn_out, [((288, 1024), F32)] * 3, (at, ffn_half, to_core(ffn_half))
    )

    *d_kv, d_query, query_line, out_grad = run(
        attend_back,
        [((512, 256), BF16)] * 4
        + [((512, 256), BF16), ((8, 128), F32), ((256, 1024), F32)],
        (at, query, keys, values, attended, inverse, w_out, starts)
        + (*d_low_parts, raw, cosine, sine, gain_tile),
        [
            pltpu.VMEM((512, 1024), BF16),
            pltpu.VMEM((2048, 128), F32),
            pltpu.VMEM((2048, 128), F32),
            pltpu.VMEM((128, 2048), BF16),
            pltpu.VMEM((512, 256), F32),
        ],
    )
    d_kv_parts = scatter(to_z, d_kv)
    d_joint, keep, send = run(
        weight_back,
        [((512, 512), BF16), ((4, 448, 256), BF16), ((4, 448, 256), BF16)],
        (at, raw, cosine, sine, gain_tile, d_query, query_line, middle_line)
        + (*d_kv_parts, x_full, out_grad),
        [pltpu.VMEM((1024, 512), F32), pltpu.VMEM((256, 128), F32)],
    )
    tail_parts = run(tail_core, [((448, 256), BF16)] * 4, (at, keep, to_core(send)))
    d_in_blocks = run(
        input_back,
        [((128, 1024), BF16)] * 4,
        (at, d_joint, w_full),
        [pltpu.VMEM((512, 1024), F32)],
    )
    *tail_blocks, tail_rows = run(
        tail_z,
        [((80, 256), BF16)] * 4 + [((128, 256), BF16)],
        (at, *scatter(to_z, tail_parts)),
        [pltpu.VMEM((448, 256), F32)],
    )
    tail_joint = jnp.concatenate(scatter(to_y, tail_blocks) + [tail_rows], axis=0)
    (tail_half,) = run(tail_x, [((448, 256), BF16)], (at, *gather(to_x, tail_joint)))
    g_query, g_key, g_value, g_out, g_gain = run(
        tail_out,
        [
            ((64, 1024), F32),
            ((64, 512), F32),
            ((64, 512), F32),
            ((64, 1024), F32),
            ((24, 128), F32),
        ],
        (at, tail_half, to_core(tail_half), gains, query_weight, key_weight, value_weight),
    )
    (tokens_grad,) = run(
        join_tokens,
        [((128, 1024), F32)],
        (at, tokens, d_middle, *scatter(to_y, d_in_blocks)),
    )
    return (
        block_output,
        tokens_grad,
        g_gain[0, 0:64],
        g_query,
        g_key,
        g_value,
        g_gain[9, 0:4],
        g_gain[10, 0:4],
        g_out,
        g_gain[8, 0:64],
        g_gate.T,
        g_up.T,
        g_down,
    )


def solution(mesh):
    return jax.shard_map(
        on_device,
        mesh=mesh,
        in_specs=(
            P(("replica", "fsdp"), None),
            P("replica", None),
            P(("replica", "fsdp"), None),
            P("fsdp"),
            P("fsdp", None),
            P("fsdp", None),
            P("fsdp", None),
            P("fsdp"),
            P("fsdp"),
            P("fsdp", None),
            P("fsdp"),
            P(None, "fsdp"),
            P(None, "fsdp"),
            P("fsdp", None),
        ),
        out_specs=(
            P(("replica", "fsdp"), None),
            P(("replica", "fsdp"), None),
            P("fsdp"),
            P("fsdp", None),
            P("fsdp", None),
            P("fsdp", None),
            P("fsdp"),
            P("fsdp"),
            P("fsdp", None),
            P("fsdp"),
            P(None, "fsdp"),
            P(None, "fsdp"),
            P("fsdp", None),
        ),
        check_vma=False,
    )
```

```python
import functools

import jax
import jax.numpy as jnp
import numpy as np
from jax import lax
from jax.experimental import pallas as pl
from jax.experimental.pallas import tpu as pltpu
from jax.sharding import PartitionSpec as P

F32 = jnp.float32
BF16 = jnp.bfloat16
EPS = 1e-05
ROPE_BASE = 1000000.0
HEAD_DIM = 64


def shape(dims, dtype):
    return jax.ShapeDtypeStruct(dims, dtype)


def run(kernel, outs, args, scratch=(), after=(), room=50):
    at, rest = args[0], args[1:]
    first, last = 1 + len(rest), 1 + len(rest) + len(after)

    def body(*refs):
        kernel(*refs[:first], *refs[last:])

    body.__name__ = kernel.__name__
    return pl.pallas_call(
        body,
        out_shape=[shape(dims, dtype) for dims, dtype in outs],
        in_specs=[pl.BlockSpec(memory_space=pltpu.SMEM)]
        + [pl.BlockSpec(memory_space=pltpu.VMEM)] * len(rest)
        + [pl.BlockSpec(memory_space=pl.ANY)] * len(after),
        out_specs=[pl.BlockSpec(memory_space=pltpu.VMEM)] * len(outs),
        scratch_shapes=list(scratch),
        compiler_params=pltpu.CompilerParams(vmem_limit_bytes=room * 1024 * 1024),
    )(at, *rest, *after)


def stacked(parts, after=()):
    rows = sum(part.shape[0] for part in parts[1:])
    return run(
        stack_rows, [((rows, parts[1].shape[1]), parts[1].dtype)], tuple(parts), after=after
    )[0]


def yz_perm(dy, dz):
    return [
        (y * 4 + z, ((y + dy) % 4) * 4 + (z + dz) % 4) for y in range(4) for z in range(4)
    ]


def to_y(value, step):
    return lax.ppermute(value, "fsdp", yz_perm(step, 0))


def to_z(value, step):
    return lax.ppermute(value, "fsdp", yz_perm(0, step))


def to_x(value, step):
    pairs = [(x * 2 + c, ((x + step) % 4) * 2 + c) for x in range(4) for c in range(2)]
    return lax.ppermute(value, "replica", pairs)


def to_core(value):
    return lax.ppermute(value, "replica", [(i, i ^ 1) for i in range(8)])


def gather(move, own):
    return [own] + [move(own, step) for step in (1, 2, 3)]


def scatter(move, blocks):
    return [blocks[0]] + [move(blocks[step], -step) for step in (1, 2, 3)]


X_GROUPS = [[x * 2 + c for x in range(4)] for c in range(2)]
Z_GROUPS = [[y * 4 + z for z in range(4)] for y in range(4)]


def sum_scatter(value, groups, axis="fsdp"):
    return lax.psum_scatter(
        value, axis, scatter_dimension=0, tiled=True, axis_index_groups=groups
    )


def all_of(value, axis, groups=None):
    return lax.all_gather(value, axis, axis=0, tiled=True, axis_index_groups=groups)


def back(place, step):
    return lax.rem(place - step + 4, 4)


def ahead(place, step):
    return lax.rem(place + step, 4)


def rows_at(start, count):
    return pl.ds(pl.multiple_of(start, count), count)


def nt(left, right):
    return lax.dot_general(left, right, (((1,), (1,)), ((), ())), preferred_element_type=F32)


def nn(left, right):
    return jnp.dot(left, right, preferred_element_type=F32)


def lane_of(value):
    return lax.broadcasted_iota(jnp.int32, value.shape, value.ndim - 1)


def low_lanes(value):
    return lane_of(value) < HEAD_DIM


def swap_halves(value):
    first = lax.rem(lane_of(value), HEAD_DIM) < HEAD_DIM // 2
    return jnp.where(first, pltpu.roll(value, 96, 1), pltpu.roll(value, 32, 1))


def head_mean(value):
    low = low_lanes(value)
    left = jnp.sum(jnp.where(low, value, 0.0), axis=1, keepdims=True)
    right = jnp.sum(jnp.where(low, 0.0, value), axis=1, keepdims=True)
    return jnp.where(low, left, right) * (1.0 / HEAD_DIM)


def head_forward(raw, gain, cosine, sine):
    normed = raw * lax.rsqrt(head_mean(raw * raw) + EPS) * gain
    return normed * cosine + swap_halves(normed) * sine


def head_backward(grad, raw, gain, cosine, sine):
    turned = grad * cosine - swap_halves(grad) * sine
    scale = lax.rsqrt(head_mean(raw * raw) + EPS)
    scaled = turned * gain
    d_raw = scale * scaled - raw * (scale * scale * scale) * head_mean(scaled * raw)
    return d_raw, jnp.sum(turned * raw * scale, axis=0, keepdims=True)


def gain_rows(tile):
    row = tile[0:8, :]
    turned = pltpu.roll(row, 64, 1)
    low = low_lanes(row)
    return jnp.where(low, row, turned)[0:1], jnp.where(low, turned, row)[0:1]


def middle_gain_row(tile):
    return jnp.concatenate([tile[8 + i : 9 + i, :] for i in range(8)], axis=1)


def stack_heads(tile, group):
    low = low_lanes(tile)
    turned = pltpu.roll(tile, 64, 1)
    if group == 0:
        pair = [jnp.where(low, tile, 0.0), jnp.where(low, turned, 0.0)]
    else:
        pair = [jnp.where(low, 0.0, turned), jnp.where(low, 0.0, tile)]
    return jnp.concatenate(pair, axis=0).astype(BF16)


def unstack_heads(stacked, group):
    top, bottom = stacked[0:128], stacked[128:256]
    low = low_lanes(top)
    if group == 0:
        return jnp.where(low, top, pltpu.roll(bottom, 64, 1))
    return jnp.where(low, pltpu.roll(top, 64, 1), bottom)


def visible_part(part, starts, place, last):
    key_place = lax.broadcasted_iota(jnp.int32, (512, 256), 0) + part * 512
    seen = key_place >= starts
    return seen & (key_place <= place) if last else seen


def row_places(block, z, starts_ref):
    place = (4 * block + z) * 128 + lax.broadcasted_iota(jnp.int32, (1, 128), 1)
    start = starts_ref[block : block + 1, :]
    return jnp.concatenate([place, place], axis=1), jnp.concatenate([start, start], axis=1)


def prepare_rows(at, rows, out):
    source = rows[...].astype(F32)
    scale = lax.rsqrt(jnp.mean(source * source, axis=1, keepdims=True) + EPS)
    out[...] = (source * scale).astype(BF16)


def place_rows(at, *refs):
    for step in range(4):
        refs[4][rows_at(back(at[0], step) * 128, 128), :] = refs[step][...]


def copy_rows(at, rows, out):
    out[...] = rows[...]


def stack_rows(at, *refs):
    out, first = refs[-1], 0
    for ref in refs[:-1]:
        out[first : first + ref.shape[0], :] = ref[...]
        first += ref.shape[0]


def join_shared(at, parts, *outs):
    for section in range(3):
        for piece in range(4):
            row, end = section * 288, section * 288 + 288
            while row < end:
                column, first = row // 128, row % 128
                count = min(128 - first, end - row)
                source = column * 512 + piece * 128 + first
                target = piece * 288 + row - section * 288
                outs[section][target : target + count, :] = parts[source : source + count, :]
                row += count


def prepare(at, gains, w_q, w_k, w_v, *sends):
    y, z = at[0], at[1]
    place = 4 * y + z
    held = gains[...]
    lane = lax.broadcasted_iota(jnp.int32, (64, 128), 1)
    line = lax.broadcasted_iota(jnp.int32, (64, 128), 0)
    column = jnp.sum(jnp.where(lane == line, held[0:1, :], 0.0), axis=1, keepdims=True)
    heads = pltpu.roll(held, 4 * place, 1)[2:3] + pltpu.roll(held, 64 + 4 * place, 1)[3:4]
    middle = pltpu.roll(held, 64 * lax.rem(place, 2), 1)[1:2]
    line = lax.broadcasted_iota(jnp.int32, (16, 128), 0)
    tile = jnp.where(line == 0, heads, 0.0) + jnp.where(line == 8 + place // 2, middle, 0.0)
    for step in range(4):
        other = ahead(y, step)
        send = sends[step]
        for source_ref, width, first in ((w_q, 256, 0), (w_k, 128, 256), (w_v, 128, 384)):
            block = source_ref[:, rows_at(other * width, width)].astype(F32) * column
            send[0:64, first : first + width] = block.astype(BF16)
        send[64:80, 0:128] = tile.astype(BF16)
        send[64:80, 128:512] = jnp.zeros((16, 384), BF16)


def project(at, *refs):
    x_full, w_parts = refs[0], refs[1:5]
    cosine_ref, sine_ref = refs[5:7]
    query, key_value, raw, w_full, gain_tile = refs[7:]
    y, z = at[0], at[1]
    total = jnp.zeros((16, 128), F32)
    for step in range(4):
        for inner in range(4):
            place = back(y, inner) * 4 + back(z, step)
            first = inner * 80
            w_full[rows_at(place * 64, 64), :] = w_parts[step][first : first + 64, :]
            total = total + w_parts[step][first + 64 : first + 80, 0:128].astype(F32)
    gain_tile[...] = total
    gain_q, gain_k = gain_rows(total)
    cosine, sine = cosine_ref[...], sine_ref[...]
    product = nn(x_full[...], w_full[...])
    raw[...] = product[:, 0:384]
    for tile in range(2):
        part = product[:, tile * 128 : tile * 128 + 128]
        turned = head_forward(part, gain_q, cosine, sine) * (HEAD_DIM**-0.5)
        query[:, tile * 128 : tile * 128 + 128] = turned.astype(BF16)
    key_value[:, 0:128] = head_forward(product[:, 256:384], gain_k, cosine, sine).astype(BF16)
    key_value[:, 128:256] = product[:, 384:512].astype(BF16)


def attend(at, query, *refs):
    kv_parts, out_parts, starts = refs[0:4], refs[4:8], refs[8]
    keys, values, attended, inverse, w_out = refs[9:14]
    partials, (values_t, mixed) = refs[14:18], refs[18:]
    y, z = at[0], at[1]
    for step in range(4):
        other = back(z, step)
        for block in range(4):
            rows = kv_parts[step][block * 128 : block * 128 + 128, :]
            target = rows_at((4 * block + other) * 128, 128)
            keys[target, :] = rows[:, 0:128]
            values[target, :] = rows[:, 128:256]
        w_out[rows_at(other * 64, 64), 0:512] = out_parts[step][320:384, :]
        w_out[rows_at(other * 64, 64), 512:1024] = out_parts[step][384:448, :]
    for part in range(4):
        chunk = values[part * 512 : part * 512 + 512, :].astype(F32)
        values_t[:, part * 512 : part * 512 + 512] = chunk.T.astype(BF16)
    for block in range(4):
        place, start = row_places(block, z, starts)
        rows = slice(block * 128, block * 128 + 128)
        for group in range(2):
            lanes = slice(group * 128, group * 128 + 128)
            stacked = stack_heads(query[rows, lanes].astype(F32), group)
            total = jnp.zeros((1, 256), F32)
            mix = jnp.zeros((128, 256), F32)
            for part in range(block + 1):
                span = slice(part * 512, part * 512 + 512)
                scores = nt(keys[span, :], stacked)
                seen = visible_part(part, start, place, part == block)
                weights = jnp.where(seen, jnp.exp(scores), 0.0)
                total = total + jnp.sum(weights, axis=0, keepdims=True)
                mix = mix + nn(values_t[:, span], weights.astype(BF16))
            share = 1.0 / total
            inverse[block * 2 + group : block * 2 + group + 1, :] = share
            attended[rows, lanes] = unstack_heads((mix * share).T, group).astype(BF16)
    mixed[...] = nn(attended[...], w_out[...])
    for step in range(4):
        partials[step][...] = mixed[rows_at(back(y, step) * 128, 128), :].astype(BF16)


def sum_parts(parts):
    total = parts[0][...].astype(F32)
    for part in parts[1:]:
        total = total + part[...].astype(F32)
    return total


def join_middle(at, rows, gain_tile, *refs):
    parts, (middle, normed) = refs[0:4], refs[4:]
    total = rows[...].astype(F32) + sum_parts(parts)
    middle[...] = total
    scale = lax.rsqrt(jnp.mean(total * total, axis=1, keepdims=True) + EPS)
    normed[...] = (total * scale * middle_gain_row(gain_tile[...])).astype(BF16)


def feed(at, *refs):
    mid_parts, ct_parts, (w_gate, w_up, w_down) = refs[0:4], refs[4:8], refs[8:11]
    blocks, (hidden, d_both), halves = refs[11:15], refs[15:17], refs[17:21]
    mid, ct, total = refs[21:]
    core = at[3]
    for step in range(4):
        mid[rows_at(back(at[0], step) * 128, 128), :] = mid_parts[step][...]
        ct[rows_at(back(at[0], step) * 128, 128), :] = ct_parts[step][...]
    for first, count in ((0, 512), (512, 512), (1024, 128)):
        rows = slice(first, first + count)
        gate = nt(mid[...], w_gate[rows, :])
        up = nt(mid[...], w_up[rows, :])
        d_hidden = nt(ct[...], w_down[rows, :])
        sigmoid = 0.5 * jnp.tanh(0.5 * gate) + 0.5
        silu = gate * sigmoid
        hidden[:, rows] = (silu * up).astype(BF16)
        d_gate = d_hidden * up * (sigmoid + silu * (1.0 - sigmoid))
        d_both[:, rows] = d_gate.astype(BF16)
        d_both[:, 1152 + first : 1152 + first + count] = (d_hidden * silu).astype(BF16)
    total[...] = nn(d_both[:, 0:1152], w_gate[...])
    total[...] += nn(d_both[:, 1152:2304], w_up[...])
    for step in range(4):
        blocks[step][...] = total[rows_at(back(at[0], step) * 128, 128), :].astype(BF16)
        lanes = slice(step * 128, step * 128 + 128)
        for which, source in enumerate((mid, ct)):
            for turn, half in enumerate((1 - core, core)):
                column = source[:, rows_at((step * 2 + half) * 128, 128)]
                halves[which * 2 + turn][:, lanes] = column


def back_middle(at, middle, cotangent, gain_tile, *refs):
    parts, (d_middle, d_low, gain_grad) = refs[0:4], refs[4:]
    grad = sum_parts(parts)
    source = middle[...]
    scale = lax.rsqrt(jnp.mean(source * source, axis=1, keepdims=True) + EPS)
    scaled = grad * middle_gain_row(gain_tile[...])
    share = jnp.mean(scaled * source, axis=1, keepdims=True)
    total = cotangent[...].astype(F32) + scale * scaled - source * (scale**3 * share)
    d_middle[...] = total
    d_low[...] = total.astype(BF16)
    line = jnp.sum(grad * source * scale, axis=0, keepdims=True)
    gain_grad[...] = jnp.broadcast_to(line, (8, 1024))


def attend_back(at, query, keys, values, attended, inverse, w_out, starts, *refs):
    d_parts, (raw, cosine_ref, sine_ref, gain_tile) = refs[0:4], refs[4:8]
    d_kv, (d_query, gain_grad, out_grad) = refs[8:12], refs[12:15]
    d_rows, d_keys, d_values, keys_t, d_mixed = refs[15:]
    y, z = at[0], at[1]
    for step in range(4):
        d_rows[rows_at(back(y, step) * 128, 128), :] = d_parts[step][...]
    d_mixed[...] = nt(d_rows[...], w_out[...]).astype(BF16).astype(F32)
    for part in range(4):
        span = slice(part * 512, part * 512 + 512)
        keys_t[:, span] = keys[span, :].astype(F32).T.astype(BF16)
    d_keys[...] = jnp.zeros((2048, 128), F32)
    d_values[...] = jnp.zeros((2048, 128), F32)
    gain_q, _ = gain_rows(gain_tile[...])
    line = jnp.zeros((1, 128), F32)
    for block in range(4):
        place, start = row_places(block, z, starts)
        rows = slice(block * 128, block * 128 + 128)
        for group in range(2):
            lanes = slice(group * 128, group * 128 + 128)
            stacked = stack_heads(query[rows, lanes].astype(F32), group)
            d_tile = d_mixed[rows, lanes]
            d_stacked = stack_heads(d_tile, group)
            product = (d_tile * attended[rows, lanes].astype(F32)).T
            delta = jnp.concatenate(
                [
                    jnp.sum(product[0:64], axis=0, keepdims=True),
                    jnp.sum(product[64:128], axis=0, keepdims=True),
                ],
                axis=1,
            )
            share = inverse[block * 2 + group : block * 2 + group + 1, :]
            d_turned = jnp.zeros((128, 256), F32)
            for part in range(block + 1):
                span = slice(part * 512, part * 512 + 512)
                scores = nt(keys[span, :], stacked)
                seen = visible_part(part, start, place, part == block)
                probs = jnp.where(seen, jnp.exp(scores) * share, 0.0)
                d_probs = nt(values[span, :], d_stacked)
                d_scores = (probs * (d_probs - delta)).astype(BF16)
                d_values[span, :] += nn(probs.astype(BF16), d_stacked)
                d_keys[span, :] += nn(d_scores, stacked)
                d_turned = d_turned + nn(keys_t[:, span], d_scores)
            d_head = unstack_heads(d_turned.T, group) * (HEAD_DIM**-0.5)
            d_raw, gain_part = head_backward(
                d_head, raw[rows, lanes], gain_q, cosine_ref[rows, :], sine_ref[rows, :]
            )
            d_query[rows, lanes] = d_raw.astype(BF16)
            line = line + gain_part
    for step in range(4):
        other = back(z, step)
        for block in range(4):
            source = rows_at((4 * block + other) * 128, 128)
            rows = slice(block * 128, block * 128 + 128)
            d_kv[step][rows, 0:128] = d_keys[source, :].astype(BF16)
            d_kv[step][rows, 128:256] = d_values[source, :].astype(BF16)
    wide = jnp.broadcast_to(line, (8, 128))
    gain_grad[...] = wide + pltpu.roll(wide, 64, 1)
    out_grad[...] = nn(attended[...].astype(F32).T.astype(BF16), d_rows[...])


def weight_back(at, raw, cosine, sine, gain_tile, d_query, query_gain, middle_gain, *refs):
    parts, (x_full, out_grad) = refs[0:4], refs[4:6]
    d_joint, keep, send = refs[6:9]
    grads, extras = refs[9:]
    z, core = at[1], at[3]
    total = sum_parts(parts)
    _, gain_k = gain_rows(gain_tile[...])
    d_key, key_line = head_backward(
        total[:, 0:128], raw[:, 256:384], gain_k, cosine[...], sine[...]
    )
    d_joint[:, 0:256] = d_query[...]
    d_joint[:, 256:384] = d_key.astype(BF16)
    d_joint[:, 384:512] = total[:, 128:256].astype(BF16)
    wide = jnp.broadcast_to(key_line, (8, 128))
    wide = wide + pltpu.roll(wide, 64, 1)
    line = lax.broadcasted_iota(jnp.int32, (16, 128), 0)
    heads_q = jnp.concatenate([query_gain[...], query_gain[...]], axis=0)
    heads_k = jnp.concatenate([wide, wide], axis=0)
    for place in range(16):
        half = middle_gain[0:8, (place // 2) * 128 : (place // 2) * 128 + 128]
        half = jnp.concatenate([half, half], axis=0)
        if place % 2:
            half = pltpu.roll(half, 64, 1)
        turn = (128 - 4 * place) % 128
        tile = jnp.where(line == 0, half, 0.0)
        tile = tile + jnp.where(line == 1, pltpu.roll(heads_q, turn, 1) if turn else heads_q, 0.0)
        tile = tile + jnp.where(line == 2, pltpu.roll(heads_k, turn, 1) if turn else heads_k, 0.0)
        extras[place * 16 : place * 16 + 16, :] = tile
    grads[...] = lax.dot_general(
        x_full[...], d_joint[...], (((0,), (0,)), ((), ())), preferred_element_type=F32
    )
    for target, which in ((send, 1 - core), (keep, core)):
        for step in range(4):
            other = back(z, step)
            for block in range(4):
                place = block * 4 + other
                first = block * 80
                target[step, first : first + 64, :] = grads[
                    rows_at(place * 64, 64), rows_at(which * 256, 256)
                ].astype(BF16)
                target[step, first + 64 : first + 80, 0:128] = extras[
                    rows_at(place * 16, 16), :
                ].astype(BF16)
                target[step, first + 64 : first + 80, 128:256] = jnp.zeros((16, 128), BF16)
            for column in range(2):
                first = 320 + 64 * column
                target[step, first : first + 64, :] = out_grad[
                    rows_at(other * 64, 64), rows_at(which * 512 + column * 256, 256)
                ].astype(BF16)


def last_back(at, d_joint, w_full, hidden, w_down, *refs):
    blocks, (grad, result) = refs[0:4], refs[4:]
    grad[...] = nt(d_joint[...], w_full[...])
    result[...] = nn(hidden[...], w_down[...])
    for step in range(4):
        rows = rows_at(back(at[0], step) * 128, 128)
        blocks[step][0:128, :] = grad[rows, :].astype(BF16)
        blocks[step][128:256, :] = result[rows, :].astype(BF16)


def join_last(at, rows, d_middle, middle, *refs):
    parts, (tokens_grad, output) = refs[0:4], refs[4:]
    total = sum_parts(parts)
    grad = total[0:128]
    source = rows[...].astype(F32)
    scale = lax.rsqrt(jnp.mean(source * source, axis=1, keepdims=True) + EPS)
    share = jnp.mean(grad * source, axis=1, keepdims=True)
    tokens_grad[...] = d_middle[...] + scale * grad - source * (scale**3 * share)
    output[...] = (middle[...] + total[128:256]).astype(BF16)


def tail_core(at, keep, received, *outs):
    for step in range(4):
        outs[step][...] = keep[step] + received[step]


def tail_z(at, *refs):
    parts, blocks, out_rows, total = refs[0:4], refs[4:8], refs[8], refs[9]
    y = at[0]
    total[...] = sum_parts(parts)
    for step in range(4):
        blocks[step][...] = total[rows_at(back(y, step) * 80, 80), :].astype(BF16)
    out_rows[...] = total[320:448, :].astype(BF16)


def tail_x(at, own, one, two, three, out):
    even = own[...].astype(F32) + two[...].astype(F32)
    odd = one[...].astype(F32) + three[...].astype(F32)
    out[...] = (even + odd).astype(BF16)


def tail_out(at, own, other, gains, w_q, w_k, w_v, g_q, g_k, g_v, g_out, g_gain):
    y, core = at[0], at[3]
    own_low = core == 0
    first = jnp.where(own_low, own[...].astype(F32), other[...].astype(F32))
    second = jnp.where(own_low, other[...].astype(F32), own[...].astype(F32))
    lane = lax.broadcasted_iota(jnp.int32, (64, 128), 1)
    line = lax.broadcasted_iota(jnp.int32, (64, 128), 0)
    column = jnp.sum(jnp.where(lane == line, gains[0:1, :], 0.0), axis=1, keepdims=True)
    products = jnp.zeros((64, 128), F32)
    extra = jnp.zeros((16, 128), F32)
    for step in range(4):
        group = ahead(y, step)
        top = step * 80
        extra = extra + first[top + 64 : top + 80, 0:128]
        for source, left, width, weight, grad in (
            (first, 0, 256, w_q, g_q),
            (second, 0, 128, w_k, g_k),
            (second, 128, 128, w_v, g_v),
        ):
            block = source[top : top + 64, left : left + width]
            where = rows_at(group * width, width)
            grad[:, where] = block * column
            product = block * weight[:, where].astype(F32)
            for tile in range(width // 128):
                products = products + product[:, tile * 128 : tile * 128 + 128]
    g_out[:, 0:256] = first[320:384]
    g_out[:, 256:512] = first[384:448]
    g_out[:, 512:768] = second[320:384]
    g_out[:, 768:1024] = second[384:448]
    sums = jnp.sum(products, axis=1, keepdims=True)
    row = jnp.sum(jnp.where(lane == line, sums, 0.0), axis=0, keepdims=True)
    g_gain[0:8, :] = jnp.broadcast_to(row, (8, 128))
    g_gain[8:24, :] = extra


def ffn_core(at, keep_a, got_a, keep_b, got_b, out):
    for first, keep, got in ((0, keep_a, got_a), (2304, keep_b, got_b)):
        for start in range(0, keep.shape[0], 288):
            rows = slice(start, start + 288)
            section, piece = (first + start) // 1152, (first + start) % 1152 // 288
            target = piece * 864 + section * 288
            for step in range(4):
                lanes = slice(step * 128, step * 128 + 128)
                out[target : target + 288, lanes] = keep[rows, lanes] + got[rows, lanes]


def ffn_order(at, rows, out):
    for column in range(4):
        out[column * 864 : column * 864 + 864, :] = rows[:, column * 128 : column * 128 + 128]


def ffn_out(at, parts, *outs):
    for section in range(3):
        for column in range(8):
            first = column * 864 + section * 288
            outs[section][:, column * 128 : column * 128 + 128] = parts[
                first : first + 288, :
            ].astype(F32)


def on_device(
    tokens,
    lengths,
    cotangent,
    attention_gain,
    query_weight,
    key_weight,
    value_weight,
    query_gain,
    key_gain,
    out_weight,
    middle_gain,
    gate_weight,
    up_weight,
    down_weight,
):
    place = lax.axis_index("fsdp")
    copy = lax.axis_index("replica")
    y, z, x, core = place // 4, place % 4, copy // 2, copy % 2
    at = jnp.stack([y, z, x, core]).astype(jnp.int32)

    def line_of(gain):
        return jnp.pad(gain.astype(F32), (0, 128 - gain.shape[0]))[None, :]

    gains = jnp.concatenate(
        [line_of(attention_gain), line_of(middle_gain), line_of(query_gain), line_of(key_gain)]
        + [jnp.zeros((4, 128), F32)],
        axis=0,
    )

    sends = run(
        prepare,
        [((80, 512), BF16)] * 4,
        (at, gains, query_weight, key_weight, value_weight),
    )
    w_rows = stacked(
        [at, sends[0]]
        + [to_y(sends[step], step) for step in (1, 2, 3)]
        + [out_weight[:, 0:512], out_weight[:, 512:1024]]
    )
    shared = jnp.concatenate(
        [gate_weight.T, up_weight.T, down_weight, jnp.zeros((160, 1024), BF16)], axis=0
    )
    shared = all_of(lax.dynamic_slice_in_dim(shared, copy * 128, 128, 0), "fsdp", Z_GROUPS)
    (normed,) = run(prepare_rows, [((128, 1024), BF16)], (at, tokens), after=(w_rows,))
    x_parts = gather(to_y, normed)
    w_parts = gather(to_z, w_rows)
    (shared,) = run(
        copy_rows, [((512, 1024), BF16)], (at, shared), after=(*w_parts[1:], *x_parts[1:])
    )
    shared = all_of(shared, "replica")

    lane = np.arange(128)
    inverse_period = ROPE_BASE ** (-2.0 * (lane % 32) / HEAD_DIM)
    sign = np.where(lane % 64 < 32, -1.0, 1.0)

    def row_starts(block, lane):
        rows = (block * 4 + z) * 128 + lane
        first, end = jnp.zeros_like(rows), jnp.zeros((), jnp.int32)
        for i in range(4):
            end = end + lengths[0, i]
            first = jnp.where(rows >= end, end, first)
        return rows, first

    _, starts = row_starts(
        lax.broadcasted_iota(jnp.int32, (8, 128), 0), lax.broadcasted_iota(jnp.int32, (8, 128), 1)
    )
    line = lax.broadcasted_iota(jnp.int32, (512, 128), 0)
    rows, first = row_starts(line // 128, line % 128)
    angles = (rows - first).astype(F32) * jnp.asarray(inverse_period, F32)
    cosine = jnp.cos(angles)
    sine = jnp.sin(angles) * jnp.asarray(sign, F32)

    (x_full,) = run(
        place_rows, [((512, 1024), BF16)], (at, *x_parts), after=(cosine, sine, starts)
    )
    query, key_value, raw, w_full, gain_tile = run(
        project,
        [
            ((512, 256), BF16),
            ((512, 256), BF16),
            ((512, 384), F32),
            ((1024, 512), BF16),
            ((16, 128), F32),
        ],
        (at, x_full, *w_parts, cosine, sine),
    )
    kv_parts = gather(to_z, key_value)
    (ct_late,) = run(copy_rows, [((128, 1024), BF16)], (at, cotangent), after=(query,))
    ct_parts = gather(to_y, ct_late)
    keys, values, attended, inverse, w_out, *mixed = run(
        attend,
        [
            ((2048, 128), BF16),
            ((2048, 128), BF16),
            ((512, 256), BF16),
            ((8, 256), F32),
            ((256, 1024), BF16),
        ]
        + [((128, 1024), BF16)] * 4,
        (at, query, *kv_parts, *w_parts, starts),
        [pltpu.VMEM((128, 2048), BF16), pltpu.VMEM((512, 1024), F32)],
        after=tuple(ct_parts[1:]),
    )
    middle, normed_mid = run(
        join_middle,
        [((128, 1024), F32), ((128, 1024), BF16)],
        (at, tokens, gain_tile, *scatter(to_y, mixed)),
    )

    w_gate, w_up, w_down = run(
        join_shared,
        [((1152, 1024), BF16)] * 3,
        (at, shared),
        after=(normed_mid,))
    *d_normed, hidden, d_both, mid_send, mid_keep, ct_send, ct_keep = run(
        feed,
        [((128, 1024), BF16)] * 4
        + [((512, 1152), BF16), ((512, 2304), BF16)]
        + [((512, 512), BF16)] * 4,
        (at, *gather(to_y, normed_mid), *ct_parts, w_gate, w_up, w_down),
        [
            pltpu.VMEM((512, 1024), BF16),
            pltpu.VMEM((512, 1024), BF16),
            pltpu.VMEM((512, 1024), F32),
        ], room=40)

    def tn(left, right):
        product = lax.dot_general(
            left, right, (((0,), (0,)), ((), ())), preferred_element_type=F32
        )
        return product.astype(BF16)

    send_a, send_b = tn(d_both, mid_send), tn(hidden, ct_send)
    got_a, got_b = to_core(send_a), to_core(send_b)
    keep_a, keep_b = tn(d_both, mid_keep), tn(hidden, ct_keep)
    d_normed_parts = scatter(to_y, d_normed)
    d_middle, d_low, middle_line = run(
        back_middle,
        [((128, 1024), F32), ((128, 1024), BF16), ((8, 1024), F32)],
        (at, middle, cotangent, gain_tile, *d_normed_parts),
        after=(keep_a, keep_b),
        room=12,
    )
    d_low_parts = gather(to_y, d_low)
    (ffn_split,) = run(
        ffn_core,
        [((3456, 512), BF16)],
        (at, keep_a, got_a, keep_b, got_b),
        after=(d_low,),
        room=20,
    )
    ffn_sum = sum_scatter(ffn_split, Z_GROUPS)
    *d_kv, d_query, query_line, out_grad = run(
        attend_back,
        [((512, 256), BF16)] * 4
        + [((512, 256), BF16), ((8, 128), F32), ((256, 1024), F32)],
        (at, query, keys, values, attended, inverse, w_out, starts)
        + (*d_low_parts, raw, cosine, sine, gain_tile),
        [
            pltpu.VMEM((512, 1024), BF16),
            pltpu.VMEM((2048, 128), F32),
            pltpu.VMEM((2048, 128), F32),
            pltpu.VMEM((128, 2048), BF16),
            pltpu.VMEM((512, 256), F32),
        ],
    )
    d_kv_parts = scatter(to_z, d_kv)
    (ffn_sum,) = run(ffn_order, [((3456, 128), BF16)], (at, ffn_sum), after=tuple(d_kv_parts[1:]))
    ffn_sum = sum_scatter(ffn_sum, X_GROUPS, "replica")
    d_joint, keep, send = run(
        weight_back,
        [((512, 512), BF16), ((4, 448, 256), BF16), ((4, 448, 256), BF16)],
        (at, raw, cosine, sine, gain_tile, d_query, query_line, middle_line)
        + (*d_kv_parts, x_full, out_grad),
        [pltpu.VMEM((1024, 512), F32), pltpu.VMEM((256, 128), F32)],
    )
    tail_parts = run(tail_core, [((448, 256), BF16)] * 4, (at, keep, to_core(send)))
    last_blocks = run(
        last_back,
        [((256, 1024), BF16)] * 4,
        (at, d_joint, w_full, hidden, w_down),
        [pltpu.VMEM((512, 1024), F32), pltpu.VMEM((512, 1024), F32)],
        after=(tail_parts[0],),
    )
    last_parts = scatter(to_y, last_blocks)
    *tail_blocks, tail_rows = run(
        tail_z,
        [((80, 256), BF16)] * 4 + [((128, 256), BF16)],
        (at, *scatter(to_z, tail_parts)),
        [pltpu.VMEM((448, 256), F32)],
        after=tuple(last_parts[1:]),
    )
    tail_joint = stacked([at, *scatter(to_y, tail_blocks), tail_rows])
    (ffn_sum,) = run(copy_rows, [((864, 128), BF16)], (at, ffn_sum), after=(tail_rows,))
    ffn_sum = all_of(ffn_sum, "replica")
    (tail_half,) = run(
        tail_x,
        [((448, 256), BF16)],
        (at, *gather(to_x, tail_joint)),
    )
    g_gate, g_up, g_down = run(
        ffn_out, [((288, 1024), F32)] * 3, (at, ffn_sum), after=(tail_half,))
    g_query, g_key, g_value, g_out, g_gain = run(
        tail_out,
        [
            ((64, 1024), F32),
            ((64, 512), F32),
            ((64, 512), F32),
            ((64, 1024), F32),
            ((24, 128), F32),
        ],
        (at, tail_half, to_core(tail_half), gains, query_weight, key_weight, value_weight),
    )
    tokens_grad, block_output = run(
        join_last,
        [((128, 1024), F32), ((128, 1024), BF16)],
        (at, tokens, d_middle, middle, *last_parts),
    )
    return (
        block_output,
        tokens_grad,
        g_gain[0, 0:64],
        g_query,
        g_key,
        g_value,
        g_gain[9, 0:4],
        g_gain[10, 0:4],
        g_out,
        g_gain[8, 0:64],
        g_gate.T,
        g_up.T,
        g_down,
    )


def solution(mesh):
    return jax.shard_map(
        on_device,
        mesh=mesh,
        in_specs=(
            P(("replica", "fsdp"), None),
            P("replica", None),
            P(("replica", "fsdp"), None),
            P("fsdp"),
            P("fsdp", None),
            P("fsdp", None),
            P("fsdp", None),
            P("fsdp"),
            P("fsdp"),
            P("fsdp", None),
            P("fsdp"),
            P(None, "fsdp"),
            P(None, "fsdp"),
            P("fsdp", None),
        ),
        out_specs=(
            P(("replica", "fsdp"), None),
            P(("replica", "fsdp"), None),
            P("fsdp"),
            P("fsdp", None),
            P("fsdp", None),
            P("fsdp", None),
            P("fsdp"),
            P("fsdp"),
            P("fsdp", None),
            P("fsdp"),
            P(None, "fsdp"),
            P(None, "fsdp"),
            P("fsdp", None),
        ),
        check_vma=False,
    )
```

```python
import functools

import jax
import jax.numpy as jnp
import numpy as np
from jax import lax
from jax.experimental import pallas as pl
from jax.experimental.pallas import tpu as pltpu
from jax.sharding import PartitionSpec as P

F32 = jnp.float32
BF16 = jnp.bfloat16
EPS = 1e-05
ROPE_BASE = 1000000.0
HEAD_DIM = 64


def shape(dims, dtype):
    return jax.ShapeDtypeStruct(dims, dtype)


def run(kernel, outs, args, scratch=(), after=(), room=50):
    at, rest = args[0], args[1:]
    first, last = 1 + len(rest), 1 + len(rest) + len(after)

    def body(*refs):
        kernel(*refs[:first], *refs[last:])

    body.__name__ = kernel.__name__
    return pl.pallas_call(
        body,
        out_shape=[shape(dims, dtype) for dims, dtype in outs],
        in_specs=[pl.BlockSpec(memory_space=pltpu.SMEM)]
        + [pl.BlockSpec(memory_space=pltpu.VMEM)] * len(rest)
        + [pl.BlockSpec(memory_space=pl.ANY)] * len(after),
        out_specs=[pl.BlockSpec(memory_space=pltpu.VMEM)] * len(outs),
        scratch_shapes=list(scratch),
        compiler_params=pltpu.CompilerParams(vmem_limit_bytes=room * 1024 * 1024),
    )(at, *rest, *after)


def stacked(parts, after=()):
    rows = sum(part.shape[0] for part in parts[1:])
    return run(
        stack_rows, [((rows, parts[1].shape[1]), parts[1].dtype)], tuple(parts), after=after
    )[0]


def yz_perm(dy, dz):
    return [
        (y * 4 + z, ((y + dy) % 4) * 4 + (z + dz) % 4) for y in range(4) for z in range(4)
    ]


def to_y(value, step):
    return lax.ppermute(value, "fsdp", yz_perm(step, 0))


def to_z(value, step):
    return lax.ppermute(value, "fsdp", yz_perm(0, step))


def to_x(value, step):
    pairs = [(x * 2 + c, ((x + step) % 4) * 2 + c) for x in range(4) for c in range(2)]
    return lax.ppermute(value, "replica", pairs)


def to_core(value):
    return lax.ppermute(value, "replica", [(i, i ^ 1) for i in range(8)])


def gather(move, own):
    return [own] + [move(own, step) for step in (1, 2, 3)]


def scatter(move, blocks):
    return [blocks[0]] + [move(blocks[step], -step) for step in (1, 2, 3)]


X_GROUPS = [[x * 2 + c for x in range(4)] for c in range(2)]
Z_GROUPS = [[y * 4 + z for z in range(4)] for y in range(4)]


def sum_scatter(value, groups, axis="fsdp"):
    return lax.psum_scatter(
        value, axis, scatter_dimension=0, tiled=True, axis_index_groups=groups
    )


def all_of(value, axis, groups=None):
    return lax.all_gather(value, axis, axis=0, tiled=True, axis_index_groups=groups)


def back(place, step):
    return lax.rem(place - step + 4, 4)


def ahead(place, step):
    return lax.rem(place + step, 4)


def rows_at(start, count):
    return pl.ds(pl.multiple_of(start, count), count)


def nt(left, right):
    return lax.dot_general(left, right, (((1,), (1,)), ((), ())), preferred_element_type=F32)


def nn(left, right):
    return jnp.dot(left, right, preferred_element_type=F32)


def lane_of(value):
    return lax.broadcasted_iota(jnp.int32, value.shape, value.ndim - 1)


def low_lanes(value):
    return lane_of(value) < HEAD_DIM


def swap_halves(value):
    first = lax.rem(lane_of(value), HEAD_DIM) < HEAD_DIM // 2
    return jnp.where(first, pltpu.roll(value, 96, 1), pltpu.roll(value, 32, 1))


def head_mean(value):
    low = low_lanes(value)
    left = jnp.sum(jnp.where(low, value, 0.0), axis=1, keepdims=True)
    right = jnp.sum(jnp.where(low, 0.0, value), axis=1, keepdims=True)
    return jnp.where(low, left, right) * (1.0 / HEAD_DIM)


def head_forward(raw, gain, cosine, sine):
    normed = raw * lax.rsqrt(head_mean(raw * raw) + EPS) * gain
    return normed * cosine + swap_halves(normed) * sine


def head_backward(grad, raw, gain, cosine, sine):
    turned = grad * cosine - swap_halves(grad) * sine
    scale = lax.rsqrt(head_mean(raw * raw) + EPS)
    scaled = turned * gain
    d_raw = scale * scaled - raw * (scale * scale * scale) * head_mean(scaled * raw)
    return d_raw, jnp.sum(turned * raw * scale, axis=0, keepdims=True)


def gain_rows(tile):
    row = tile[0:8, :]
    turned = pltpu.roll(row, 64, 1)
    low = low_lanes(row)
    return jnp.where(low, row, turned)[0:1], jnp.where(low, turned, row)[0:1]


def middle_gain_row(tile):
    return jnp.concatenate([tile[8 + i : 9 + i, :] for i in range(8)], axis=1)


def stack_heads(tile, group):
    low = low_lanes(tile)
    turned = pltpu.roll(tile, 64, 1)
    if group == 0:
        pair = [jnp.where(low, tile, 0.0), jnp.where(low, turned, 0.0)]
    else:
        pair = [jnp.where(low, 0.0, turned), jnp.where(low, 0.0, tile)]
    return jnp.concatenate(pair, axis=0).astype(BF16)


def unstack_heads(stacked, group):
    top, bottom = stacked[0:128], stacked[128:256]
    low = low_lanes(top)
    if group == 0:
        return jnp.where(low, top, pltpu.roll(bottom, 64, 1))
    return jnp.where(low, pltpu.roll(top, 64, 1), bottom)


def visible_part(part, starts, place, last):
    key_place = lax.broadcasted_iota(jnp.int32, (512, 256), 0) + part * 512
    seen = key_place >= starts
    return seen & (key_place <= place) if last else seen


def row_places(block, z, starts_ref):
    place = (4 * block + z) * 128 + lax.broadcasted_iota(jnp.int32, (1, 128), 1)
    start = starts_ref[block : block + 1, :]
    return jnp.concatenate([place, place], axis=1), jnp.concatenate([start, start], axis=1)


def prepare_rows(at, rows, out):
    source = rows[...].astype(F32)
    scale = lax.rsqrt(jnp.mean(source * source, axis=1, keepdims=True) + EPS)
    out[...] = (source * scale).astype(BF16)


def place_rows(at, *refs):
    for step in range(4):
        refs[4][rows_at(back(at[0], step) * 128, 128), :] = refs[step][...]


def copy_rows(at, rows, out):
    out[...] = rows[...]


def stack_rows(at, *refs):
    out, first = refs[-1], 0
    for ref in refs[:-1]:
        out[first : first + ref.shape[0], :] = ref[...]
        first += ref.shape[0]


def join_shared(at, parts, *outs):
    for section in range(3):
        for piece in range(4):
            row, end = section * 288, section * 288 + 288
            while row < end:
                column, first = row // 128, row % 128
                count = min(128 - first, end - row)
                source = column * 512 + piece * 128 + first
                target = piece * 288 + row - section * 288
                outs[section][target : target + count, :] = parts[source : source + count, :]
                row += count


def prepare(at, gains, w_q, w_k, w_v, *sends):
    y, z = at[0], at[1]
    place = 4 * y + z
    held = gains[...]
    lane = lax.broadcasted_iota(jnp.int32, (64, 128), 1)
    line = lax.broadcasted_iota(jnp.int32, (64, 128), 0)
    column = jnp.sum(jnp.where(lane == line, held[0:1, :], 0.0), axis=1, keepdims=True)
    heads = pltpu.roll(held, 4 * place, 1)[2:3] + pltpu.roll(held, 64 + 4 * place, 1)[3:4]
    middle = pltpu.roll(held, 64 * lax.rem(place, 2), 1)[1:2]
    line = lax.broadcasted_iota(jnp.int32, (16, 128), 0)
    tile = jnp.where(line == 0, heads, 0.0) + jnp.where(line == 8 + place // 2, middle, 0.0)
    for step in range(4):
        other = ahead(y, step)
        send = sends[step]
        for source_ref, width, first in ((w_q, 256, 0), (w_k, 128, 256), (w_v, 128, 384)):
            block = source_ref[:, rows_at(other * width, width)].astype(F32) * column
            send[0:64, first : first + width] = block.astype(BF16)
        send[64:80, 0:128] = tile.astype(BF16)
        send[64:80, 128:512] = jnp.zeros((16, 384), BF16)


def project(at, *refs):
    x_full, w_parts = refs[0], refs[1:5]
    cosine_ref, sine_ref = refs[5:7]
    query, key_value, raw, w_full, gain_tile = refs[7:]
    y, z = at[0], at[1]
    total = jnp.zeros((16, 128), F32)
    for step in range(4):
        for inner in range(4):
            place = back(y, inner) * 4 + back(z, step)
            first = inner * 80
            w_full[rows_at(place * 64, 64), :] = w_parts[step][first : first + 64, :]
            total = total + w_parts[step][first + 64 : first + 80, 0:128].astype(F32)
    gain_tile[...] = total
    gain_q, gain_k = gain_rows(total)
    cosine, sine = cosine_ref[...], sine_ref[...]
    product = nn(x_full[...], w_full[...])
    raw[...] = product[:, 0:384]
    for tile in range(2):
        part = product[:, tile * 128 : tile * 128 + 128]
        turned = head_forward(part, gain_q, cosine, sine) * (HEAD_DIM**-0.5)
        query[:, tile * 128 : tile * 128 + 128] = turned.astype(BF16)
    key_value[:, 0:128] = head_forward(product[:, 256:384], gain_k, cosine, sine).astype(BF16)
    key_value[:, 128:256] = product[:, 384:512].astype(BF16)


def attend(at, query, *refs):
    kv_parts, out_parts, starts = refs[0:4], refs[4:8], refs[8]
    keys, values, attended, inverse, w_out = refs[9:14]
    partials, (values_t, mixed) = refs[14:18], refs[18:]
    y, z = at[0], at[1]
    for step in range(4):
        other = back(z, step)
        for block in range(4):
            rows = kv_parts[step][block * 128 : block * 128 + 128, :]
            target = rows_at((4 * block + other) * 128, 128)
            keys[target, :] = rows[:, 0:128]
            values[target, :] = rows[:, 128:256]
        w_out[rows_at(other * 64, 64), 0:512] = out_parts[step][320:384, :]
        w_out[rows_at(other * 64, 64), 512:1024] = out_parts[step][384:448, :]
    for part in range(4):
        chunk = values[part * 512 : part * 512 + 512, :].astype(F32)
        values_t[:, part * 512 : part * 512 + 512] = chunk.T.astype(BF16)
    for block in range(4):
        place, start = row_places(block, z, starts)
        rows = slice(block * 128, block * 128 + 128)
        for group in range(2):
            lanes = slice(group * 128, group * 128 + 128)
            stacked = stack_heads(query[rows, lanes].astype(F32), group)
            total = jnp.zeros((1, 256), F32)
            mix = jnp.zeros((128, 256), F32)
            for part in range(block + 1):
                span = slice(part * 512, part * 512 + 512)
                scores = nt(keys[span, :], stacked)
                seen = visible_part(part, start, place, part == block)
                weights = jnp.where(seen, jnp.exp(scores), 0.0)
                total = total + jnp.sum(weights, axis=0, keepdims=True)
                mix = mix + nn(values_t[:, span], weights.astype(BF16))
            share = 1.0 / total
            inverse[block * 2 + group : block * 2 + group + 1, :] = share
            attended[rows, lanes] = unstack_heads((mix * share).T, group).astype(BF16)
    mixed[...] = nn(attended[...], w_out[...])
    for step in range(4):
        partials[step][...] = mixed[rows_at(back(y, step) * 128, 128), :].astype(BF16)


def sum_parts(parts):
    total = parts[0][...].astype(F32)
    for part in parts[1:]:
        total = total + part[...].astype(F32)
    return total


def join_middle(at, rows, gain_tile, *refs):
    parts, (middle, normed) = refs[0:4], refs[4:]
    total = rows[...].astype(F32) + sum_parts(parts)
    middle[...] = total
    scale = lax.rsqrt(jnp.mean(total * total, axis=1, keepdims=True) + EPS)
    normed[...] = (total * scale * middle_gain_row(gain_tile[...])).astype(BF16)


def feed(at, *refs):
    mid_parts, ct_parts, (w_gate, w_up, w_down) = refs[0:4], refs[4:8], refs[8:11]
    blocks, (hidden, d_both), halves = refs[11:15], refs[15:17], refs[17:21]
    mid, ct, total = refs[21:]
    core = at[3]
    for step in range(4):
        mid[rows_at(back(at[0], step) * 128, 128), :] = mid_parts[step][...]
        ct[rows_at(back(at[0], step) * 128, 128), :] = ct_parts[step][...]
    for first, count in ((0, 512), (512, 512), (1024, 128)):
        rows = slice(first, first + count)
        gate = nt(mid[...], w_gate[rows, :])
        up = nt(mid[...], w_up[rows, :])
        d_hidden = nt(ct[...], w_down[rows, :])
        sigmoid = 0.5 * jnp.tanh(0.5 * gate) + 0.5
        silu = gate * sigmoid
        hidden[:, rows] = (silu * up).astype(BF16)
        d_gate = d_hidden * up * (sigmoid + silu * (1.0 - sigmoid))
        d_both[:, rows] = d_gate.astype(BF16)
        d_both[:, 1152 + first : 1152 + first + count] = (d_hidden * silu).astype(BF16)
    total[...] = nn(d_both[:, 0:1152], w_gate[...])
    total[...] += nn(d_both[:, 1152:2304], w_up[...])
    for step in range(4):
        blocks[step][...] = total[rows_at(back(at[0], step) * 128, 128), :].astype(BF16)
        lanes = slice(step * 128, step * 128 + 128)
        for which, source in enumerate((mid, ct)):
            for turn, half in enumerate((1 - core, core)):
                column = source[:, rows_at((step * 2 + half) * 128, 128)]
                halves[which * 2 + turn][:, lanes] = column


def back_middle(at, middle, cotangent, gain_tile, *refs):
    parts, (d_middle, d_low, gain_grad) = refs[0:4], refs[4:]
    grad = sum_parts(parts)
    source = middle[...]
    scale = lax.rsqrt(jnp.mean(source * source, axis=1, keepdims=True) + EPS)
    scaled = grad * middle_gain_row(gain_tile[...])
    share = jnp.mean(scaled * source, axis=1, keepdims=True)
    total = cotangent[...].astype(F32) + scale * scaled - source * (scale**3 * share)
    d_middle[...] = total
    d_low[...] = total.astype(BF16)
    line = jnp.sum(grad * source * scale, axis=0, keepdims=True)
    gain_grad[...] = jnp.broadcast_to(line, (8, 1024))


def attend_back(at, query, keys, values, attended, inverse, w_out, starts, *refs):
    d_parts, (raw, cosine_ref, sine_ref, gain_tile) = refs[0:4], refs[4:8]
    d_kv, (d_query, gain_grad, out_grad) = refs[8:12], refs[12:15]
    d_rows, d_keys, d_values, keys_t, d_mixed = refs[15:]
    y, z = at[0], at[1]
    for step in range(4):
        d_rows[rows_at(back(y, step) * 128, 128), :] = d_parts[step][...]
    d_mixed[...] = nt(d_rows[...], w_out[...]).astype(BF16).astype(F32)
    for part in range(4):
        span = slice(part * 512, part * 512 + 512)
        keys_t[:, span] = keys[span, :].astype(F32).T.astype(BF16)
    d_keys[...] = jnp.zeros((2048, 128), F32)
    d_values[...] = jnp.zeros((2048, 128), F32)
    gain_q, _ = gain_rows(gain_tile[...])
    line = jnp.zeros((1, 128), F32)
    for block in range(4):
        place, start = row_places(block, z, starts)
        rows = slice(block * 128, block * 128 + 128)
        for group in range(2):
            lanes = slice(group * 128, group * 128 + 128)
            stacked = stack_heads(query[rows, lanes].astype(F32), group)
            d_tile = d_mixed[rows, lanes]
            d_stacked = stack_heads(d_tile, group)
            product = (d_tile * attended[rows, lanes].astype(F32)).T
            delta = jnp.concatenate(
                [
                    jnp.sum(product[0:64], axis=0, keepdims=True),
                    jnp.sum(product[64:128], axis=0, keepdims=True),
                ],
                axis=1,
            )
            share = inverse[block * 2 + group : block * 2 + group + 1, :]
            d_turned = jnp.zeros((128, 256), F32)
            for part in range(block + 1):
                span = slice(part * 512, part * 512 + 512)
                scores = nt(keys[span, :], stacked)
                seen = visible_part(part, start, place, part == block)
                probs = jnp.where(seen, jnp.exp(scores) * share, 0.0)
                d_probs = nt(values[span, :], d_stacked)
                d_scores = (probs * (d_probs - delta)).astype(BF16)
                d_values[span, :] += nn(probs.astype(BF16), d_stacked)
                d_keys[span, :] += nn(d_scores, stacked)
                d_turned = d_turned + nn(keys_t[:, span], d_scores)
            d_head = unstack_heads(d_turned.T, group) * (HEAD_DIM**-0.5)
            d_raw, gain_part = head_backward(
                d_head, raw[rows, lanes], gain_q, cosine_ref[rows, :], sine_ref[rows, :]
            )
            d_query[rows, lanes] = d_raw.astype(BF16)
            line = line + gain_part
    for step in range(4):
        other = back(z, step)
        for block in range(4):
            source = rows_at((4 * block + other) * 128, 128)
            rows = slice(block * 128, block * 128 + 128)
            d_kv[step][rows, 0:128] = d_keys[source, :].astype(BF16)
            d_kv[step][rows, 128:256] = d_values[source, :].astype(BF16)
    wide = jnp.broadcast_to(line, (8, 128))
    gain_grad[...] = wide + pltpu.roll(wide, 64, 1)
    out_grad[...] = nn(attended[...].astype(F32).T.astype(BF16), d_rows[...])


def weight_back(at, raw, cosine, sine, gain_tile, d_query, query_gain, middle_gain, *refs):
    parts, (x_full, out_grad) = refs[0:4], refs[4:6]
    d_joint, keep, send = refs[6:9]
    grads, extras = refs[9:]
    z, core = at[1], at[3]
    total = sum_parts(parts)
    _, gain_k = gain_rows(gain_tile[...])
    d_key, key_line = head_backward(
        total[:, 0:128], raw[:, 256:384], gain_k, cosine[...], sine[...]
    )
    d_joint[:, 0:256] = d_query[...]
    d_joint[:, 256:384] = d_key.astype(BF16)
    d_joint[:, 384:512] = total[:, 128:256].astype(BF16)
    wide = jnp.broadcast_to(key_line, (8, 128))
    wide = wide + pltpu.roll(wide, 64, 1)
    line = lax.broadcasted_iota(jnp.int32, (16, 128), 0)
    heads_q = jnp.concatenate([query_gain[...], query_gain[...]], axis=0)
    heads_k = jnp.concatenate([wide, wide], axis=0)
    for place in range(16):
        half = middle_gain[0:8, (place // 2) * 128 : (place // 2) * 128 + 128]
        half = jnp.concatenate([half, half], axis=0)
        if place % 2:
            half = pltpu.roll(half, 64, 1)
        turn = (128 - 4 * place) % 128
        tile = jnp.where(line == 0, half, 0.0)
        tile = tile + jnp.where(line == 1, pltpu.roll(heads_q, turn, 1) if turn else heads_q, 0.0)
        tile = tile + jnp.where(line == 2, pltpu.roll(heads_k, turn, 1) if turn else heads_k, 0.0)
        extras[place * 16 : place * 16 + 16, :] = tile
    grads[...] = lax.dot_general(
        x_full[...], d_joint[...], (((0,), (0,)), ((), ())), preferred_element_type=F32
    )
    for target, which in ((send, 1 - core), (keep, core)):
        for step in range(4):
            other = back(z, step)
            for block in range(4):
                place = block * 4 + other
                first = block * 80
                target[step, first : first + 64, :] = grads[
                    rows_at(place * 64, 64), rows_at(which * 256, 256)
                ].astype(BF16)
                target[step, first + 64 : first + 80, 0:128] = extras[
                    rows_at(place * 16, 16), :
                ].astype(BF16)
                target[step, first + 64 : first + 80, 128:256] = jnp.zeros((16, 128), BF16)
            for column in range(2):
                first = 320 + 64 * column
                target[step, first : first + 64, :] = out_grad[
                    rows_at(other * 64, 64), rows_at(which * 512 + column * 256, 256)
                ].astype(BF16)


def last_back(at, d_joint, w_full, hidden, w_down, *refs):
    blocks, (grad, result) = refs[0:4], refs[4:]
    grad[...] = nt(d_joint[...], w_full[...])
    result[...] = nn(hidden[...], w_down[...])
    for step in range(4):
        rows = rows_at(back(at[0], step) * 128, 128)
        blocks[step][0:128, :] = grad[rows, :].astype(BF16)
        blocks[step][128:256, :] = result[rows, :].astype(BF16)


def join_last(at, rows, d_middle, middle, *refs):
    parts, (tokens_grad, output) = refs[0:4], refs[4:]
    total = sum_parts(parts)
    grad = total[0:128]
    source = rows[...].astype(F32)
    scale = lax.rsqrt(jnp.mean(source * source, axis=1, keepdims=True) + EPS)
    share = jnp.mean(grad * source, axis=1, keepdims=True)
    tokens_grad[...] = d_middle[...] + scale * grad - source * (scale**3 * share)
    output[...] = (middle[...] + total[128:256]).astype(BF16)


def tail_core(at, keep, received, *outs):
    for step in range(4):
        outs[step][...] = keep[step] + received[step]


def tail_z(at, *refs):
    parts, blocks, out_rows, total = refs[0:4], refs[4:8], refs[8], refs[9]
    y = at[0]
    total[...] = sum_parts(parts)
    for step in range(4):
        blocks[step][...] = total[rows_at(back(y, step) * 80, 80), :].astype(BF16)
    out_rows[...] = total[320:448, :].astype(BF16)


def tail_x(at, own, one, two, three, out):
    even = own[...].astype(F32) + two[...].astype(F32)
    odd = one[...].astype(F32) + three[...].astype(F32)
    out[...] = (even + odd).astype(BF16)


def tail_out(at, own, other, gains, w_q, w_k, w_v, g_q, g_k, g_v, g_out, g_gain):
    y, core = at[0], at[3]
    own_low = core == 0
    first = jnp.where(own_low, own[...].astype(F32), other[...].astype(F32))
    second = jnp.where(own_low, other[...].astype(F32), own[...].astype(F32))
    lane = lax.broadcasted_iota(jnp.int32, (64, 128), 1)
    line = lax.broadcasted_iota(jnp.int32, (64, 128), 0)
    column = jnp.sum(jnp.where(lane == line, gains[0:1, :], 0.0), axis=1, keepdims=True)
    products = jnp.zeros((64, 128), F32)
    extra = jnp.zeros((16, 128), F32)
    for step in range(4):
        group = ahead(y, step)
        top = step * 80
        extra = extra + first[top + 64 : top + 80, 0:128]
        for source, left, width, weight, grad in (
            (first, 0, 256, w_q, g_q),
            (second, 0, 128, w_k, g_k),
            (second, 128, 128, w_v, g_v),
        ):
            block = source[top : top + 64, left : left + width]
            where = rows_at(group * width, width)
            grad[:, where] = block * column
            product = block * weight[:, where].astype(F32)
            for tile in range(width // 128):
                products = products + product[:, tile * 128 : tile * 128 + 128]
    g_out[:, 0:256] = first[320:384]
    g_out[:, 256:512] = first[384:448]
    g_out[:, 512:768] = second[320:384]
    g_out[:, 768:1024] = second[384:448]
    sums = jnp.sum(products, axis=1, keepdims=True)
    row = jnp.sum(jnp.where(lane == line, sums, 0.0), axis=0, keepdims=True)
    g_gain[0:8, :] = jnp.broadcast_to(row, (8, 128))
    g_gain[8:24, :] = extra


def ffn_core(at, keep_a, got_a, keep_b, got_b, out):
    for first, keep, got in ((0, keep_a, got_a), (2304, keep_b, got_b)):
        for start in range(0, keep.shape[0], 288):
            rows = slice(start, start + 288)
            section, piece = (first + start) // 1152, (first + start) % 1152 // 288
            target = piece * 864 + section * 288
            for step in range(4):
                lanes = slice(step * 128, step * 128 + 128)
                out[target : target + 288, lanes] = keep[rows, lanes] + got[rows, lanes]


def ffn_order(at, rows, out):
    for column in range(4):
        out[column * 864 : column * 864 + 864, :] = rows[:, column * 128 : column * 128 + 128]


def ffn_out(at, parts, *outs):
    for section in range(3):
        for column in range(8):
            first = column * 864 + section * 288
            outs[section][:, column * 128 : column * 128 + 128] = parts[
                first : first + 288, :
            ].astype(F32)


def on_device(
    tokens,
    lengths,
    cotangent,
    attention_gain,
    query_weight,
    key_weight,
    value_weight,
    query_gain,
    key_gain,
    out_weight,
    middle_gain,
    gate_weight,
    up_weight,
    down_weight,
):
    place = lax.axis_index("fsdp")
    copy = lax.axis_index("replica")
    y, z, x, core = place // 4, place % 4, copy // 2, copy % 2
    at = jnp.stack([y, z, x, core]).astype(jnp.int32)

    def line_of(gain):
        return jnp.pad(gain.astype(F32), (0, 128 - gain.shape[0]))[None, :]

    gains = jnp.concatenate(
        [line_of(attention_gain), line_of(middle_gain), line_of(query_gain), line_of(key_gain)]
        + [jnp.zeros((4, 128), F32)],
        axis=0,
    )

    sends = run(
        prepare,
        [((80, 512), BF16)] * 4,
        (at, gains, query_weight, key_weight, value_weight),
    )
    w_rows = stacked(
        [at, sends[0]]
        + [to_y(sends[step], step) for step in (1, 2, 3)]
        + [out_weight[:, 0:512], out_weight[:, 512:1024]]
    )
    shared = jnp.concatenate(
        [gate_weight.T, up_weight.T, down_weight, jnp.zeros((160, 1024), BF16)], axis=0
    )
    shared = all_of(lax.dynamic_slice_in_dim(shared, copy * 128, 128, 0), "fsdp", Z_GROUPS)
    (normed,) = run(prepare_rows, [((128, 1024), BF16)], (at, tokens), after=(w_rows,))
    x_parts = gather(to_y, normed)
    w_parts = gather(to_z, w_rows)
    (shared,) = run(
        copy_rows, [((512, 1024), BF16)], (at, shared), after=(*w_parts[1:], *x_parts[1:])
    )
    shared = all_of(shared, "replica")

    lane = np.arange(128)
    inverse_period = ROPE_BASE ** (-2.0 * (lane % 32) / HEAD_DIM)
    sign = np.where(lane % 64 < 32, -1.0, 1.0)

    def row_starts(block, lane):
        rows = (block * 4 + z) * 128 + lane
        first, end = jnp.zeros_like(rows), jnp.zeros((), jnp.int32)
        for i in range(4):
            end = end + lengths[0, i]
            first = jnp.where(rows >= end, end, first)
        return rows, first

    _, starts = row_starts(
        lax.broadcasted_iota(jnp.int32, (8, 128), 0), lax.broadcasted_iota(jnp.int32, (8, 128), 1)
    )
    line = lax.broadcasted_iota(jnp.int32, (512, 128), 0)
    rows, first = row_starts(line // 128, line % 128)
    angles = (rows - first).astype(F32) * jnp.asarray(inverse_period, F32)
    cosine = jnp.cos(angles)
    sine = jnp.sin(angles) * jnp.asarray(sign, F32)

    (x_full,) = run(
        place_rows, [((512, 1024), BF16)], (at, *x_parts), after=(cosine, sine, starts)
    )
    query, key_value, raw, w_full, gain_tile = run(
        project,
        [
            ((512, 256), BF16),
            ((512, 256), BF16),
            ((512, 384), F32),
            ((1024, 512), BF16),
            ((16, 128), F32),
        ],
        (at, x_full, *w_parts, cosine, sine),
    )
    kv_parts = gather(to_z, key_value)
    (ct_late,) = run(copy_rows, [((128, 1024), BF16)], (at, cotangent), after=(query,))
    ct_parts = gather(to_y, ct_late)
    keys, values, attended, inverse, w_out, *mixed = run(
        attend,
        [
            ((2048, 128), BF16),
            ((2048, 128), BF16),
            ((512, 256), BF16),
            ((8, 256), F32),
            ((256, 1024), BF16),
        ]
        + [((128, 1024), BF16)] * 4,
        (at, query, *kv_parts, *w_parts, starts),
        [pltpu.VMEM((128, 2048), BF16), pltpu.VMEM((512, 1024), F32)],
        after=tuple(ct_parts[1:]),
    )
    middle, normed_mid = run(
        join_middle,
        [((128, 1024), F32), ((128, 1024), BF16)],
        (at, tokens, gain_tile, *scatter(to_y, mixed)),
    )

    w_gate, w_up, w_down = run(
        join_shared,
        [((1152, 1024), BF16)] * 3,
        (at, shared),
        after=(normed_mid,))
    *d_normed, hidden, d_both, mid_send, mid_keep, ct_send, ct_keep = run(
        feed,
        [((128, 1024), BF16)] * 4
        + [((512, 1152), BF16), ((512, 2304), BF16)]
        + [((512, 512), BF16)] * 4,
        (at, *gather(to_y, normed_mid), *ct_parts, w_gate, w_up, w_down),
        [
            pltpu.VMEM((512, 1024), BF16),
            pltpu.VMEM((512, 1024), BF16),
            pltpu.VMEM((512, 1024), F32),
        ], room=40)

    def tn(left, right):
        product = lax.dot_general(
            left, right, (((0,), (0,)), ((), ())), preferred_element_type=F32
        )
        return product.astype(BF16)

    send_a, send_b = tn(d_both, mid_send), tn(hidden, ct_send)
    got_a, got_b = to_core(send_a), to_core(send_b)
    keep_a, keep_b = tn(d_both, mid_keep), tn(hidden, ct_keep)
    d_normed_parts = scatter(to_y, d_normed)
    d_middle, d_low, middle_line = run(
        back_middle,
        [((128, 1024), F32), ((128, 1024), BF16), ((8, 1024), F32)],
        (at, middle, cotangent, gain_tile, *d_normed_parts),
        after=(keep_a, keep_b),
        room=12,
    )
    d_low_parts = gather(to_y, d_low)
    (ffn_split,) = run(
        ffn_core,
        [((3456, 512), BF16)],
        (at, keep_a, got_a, keep_b, got_b),
        after=(d_low,),
        room=20,
    )
    ffn_sum = sum_scatter(ffn_split, Z_GROUPS)
    *d_kv, d_query, query_line, out_grad = run(
        attend_back,
        [((512, 256), BF16)] * 4
        + [((512, 256), BF16), ((8, 128), F32), ((256, 1024), F32)],
        (at, query, keys, values, attended, inverse, w_out, starts)
        + (*d_low_parts, raw, cosine, sine, gain_tile),
        [
            pltpu.VMEM((512, 1024), BF16),
            pltpu.VMEM((2048, 128), F32),
            pltpu.VMEM((2048, 128), F32),
            pltpu.VMEM((128, 2048), BF16),
            pltpu.VMEM((512, 256), F32),
        ],
    )
    d_kv_parts = scatter(to_z, d_kv)
    d_joint, keep, send = run(
        weight_back,
        [((512, 512), BF16), ((4, 448, 256), BF16), ((4, 448, 256), BF16)],
        (at, raw, cosine, sine, gain_tile, d_query, query_line, middle_line)
        + (*d_kv_parts, x_full, out_grad),
        [pltpu.VMEM((1024, 512), F32), pltpu.VMEM((256, 128), F32)],
    )
    (ffn_sum,) = run(ffn_order, [((3456, 128), BF16)], (at, ffn_sum), after=(d_joint,))
    ffn_sum = sum_scatter(ffn_sum, X_GROUPS, "replica")
    tail_parts = run(tail_core, [((448, 256), BF16)] * 4, (at, keep, to_core(send)))
    last_blocks = run(
        last_back,
        [((256, 1024), BF16)] * 4,
        (at, d_joint, w_full, hidden, w_down),
        [pltpu.VMEM((512, 1024), F32), pltpu.VMEM((512, 1024), F32)],
    )
    last_parts = scatter(to_y, last_blocks)
    *tail_blocks, tail_rows = run(
        tail_z,
        [((80, 256), BF16)] * 4 + [((128, 256), BF16)],
        (at, *scatter(to_z, tail_parts)),
        [pltpu.VMEM((448, 256), F32)],
        after=tuple(last_parts[1:]),
    )
    tail_joint = stacked([at, *scatter(to_y, tail_blocks), tail_rows])
    (ffn_sum,) = run(copy_rows, [((864, 128), BF16)], (at, ffn_sum), after=(tail_rows,))
    ffn_sum = all_of(ffn_sum, "replica")
    (tail_half,) = run(
        tail_x,
        [((448, 256), BF16)],
        (at, *gather(to_x, tail_joint)),
    )
    g_gate, g_up, g_down = run(
        ffn_out, [((288, 1024), F32)] * 3, (at, ffn_sum), after=(tail_half,))
    g_query, g_key, g_value, g_out, g_gain = run(
        tail_out,
        [
            ((64, 1024), F32),
            ((64, 512), F32),
            ((64, 512), F32),
            ((64, 1024), F32),
            ((24, 128), F32),
        ],
        (at, tail_half, to_core(tail_half), gains, query_weight, key_weight, value_weight),
    )
    tokens_grad, block_output = run(
        join_last,
        [((128, 1024), F32), ((128, 1024), BF16)],
        (at, tokens, d_middle, middle, *last_parts),
    )
    return (
        block_output,
        tokens_grad,
        g_gain[0, 0:64],
        g_query,
        g_key,
        g_value,
        g_gain[9, 0:4],
        g_gain[10, 0:4],
        g_out,
        g_gain[8, 0:64],
        g_gate.T,
        g_up.T,
        g_down,
    )


def solution(mesh):
    return jax.shard_map(
        on_device,
        mesh=mesh,
        in_specs=(
            P(("replica", "fsdp"), None),
            P("replica", None),
            P(("replica", "fsdp"), None),
            P("fsdp"),
            P("fsdp", None),
            P("fsdp", None),
            P("fsdp", None),
            P("fsdp"),
            P("fsdp"),
            P("fsdp", None),
            P("fsdp"),
            P(None, "fsdp"),
            P(None, "fsdp"),
            P("fsdp", None),
        ),
        out_specs=(
            P(("replica", "fsdp"), None),
            P(("replica", "fsdp"), None),
            P("fsdp"),
            P("fsdp", None),
            P("fsdp", None),
            P("fsdp", None),
            P("fsdp"),
            P("fsdp"),
            P("fsdp", None),
            P("fsdp"),
            P(None, "fsdp"),
            P(None, "fsdp"),
            P("fsdp", None),
        ),
        check_vma=False,
    )
```
